128 devices in a mesh: layer: 4 (over x_lo, core), tile: 32 (over z, x_hi, y).
Axes of the slice: x: 4 (x_hi: 2, x_lo: 2; x = x_hi * 2 + x_lo), y: 4, z: 4, core: 2. Of those that a mesh axis runs over, the one named last changes fastest.
Arguments:
- load_current: float32 [8, 4096, 2816], P('layer', 'tile'), may hold values from 0.05 to 1
- metal_class: int32 [8, 4096, 2816], P('layer', 'tile'), may hold values from 0 to 15
- via_mask: int32 [8, 4096, 2816], P('layer', 'tile'), may hold values 0 or 1
- temp_prior: float32 [8, 4096, 2816], P('layer', 'tile'), may hold values from 25 to 125
- drop_prior: float32 [8, 4096, 2816], P('layer', 'tile'), may hold values from 0 to 1
- class_conductance: float32 [8, 16], P('layer'), may hold values from 0.5 to 8
Outputs:
- drop_next: float32 [8, 4096, 2816], P('layer', 'tile')
- temp_rise: float32 [8, 4096, 2816], P('layer', 'tile')
The draws below stay inside these ranges and needn't reach their ends.
Inputs may be any that keep to these rules, and one draw needn't show every extreme that they name: `metal_class`: class indices.
All inputs are finite; a program needn't handle non-finite values. No bound on the sum of `via_mask` on one device may be relied on, other than what follows from the above.
Results may differ from the reference program's by a relative error of at most 0.0003.
Values sent between devices are 32-bit elements; how exact they have to be, the bound alone decides.
A program may use at most 192 MiB of HBM per device.

```python
import math
import jax
import jax.numpy as jnp

COLS = 2816
CLASSES = 16
LAYERS = 8
GRID_ROWS = 4096


def with_ends(array, rng, low, top_value):
    longest = array.shape.index(max(array.shape))
    spots = []
    for shift in (0, 1):
        where = [jax.random.randint(jax.random.fold_in(rng, axis), (), 0, length) for axis, length in enumerate(array.shape)]
        where[longest] = (where[longest] + shift) % array.shape[longest]
        spots.append(tuple(where))
    return array.at[spots[0]].set(low).at[spots[1]].set(top_value)


def levels(rng, dims, split, smallest, top_value):
    factor_of = 1.0
    for dim, blocks in split:
        steps = jax.random.uniform(jax.random.fold_in(jax.random.fold_in(rng, 6), dim), (blocks,), jnp.float32, smallest / len(split), top_value / len(split))
        factor_of = factor_of * jnp.repeat(jnp.exp(steps), dims[dim] // blocks).reshape((-1,) + (1,) * (len(dims) - 1 - dim))
    return factor_of


def setup_inputs(seed: int = 0) -> dict:
    splits = jax.random.split(jax.random.key(seed), 7)
    return {
        "load_current": jnp.clip(jnp.exp(math.log(1.0) - 2.9957323 * jax.random.uniform(splits[0], (LAYERS, GRID_ROWS, COLS), jnp.float32) ** levels(splits[0], (LAYERS, GRID_ROWS, COLS), ((0, 4), (1, 32)), -0.2, 0.2)), 0.05, 1.0),
        "metal_class": with_ends(jax.random.randint(splits[1], (LAYERS, GRID_ROWS, COLS), 0, CLASSES), jax.random.fold_in(splits[1], 1), 0, CLASSES - 1).astype(jnp.int32),
        "via_mask": with_ends((jax.random.randint(splits[2], (LAYERS, GRID_ROWS, COLS), 0, 4) < 1).astype(jnp.int32), jax.random.fold_in(splits[2], 1), 0, 1),
        "temp_prior": jnp.clip(25.0 + 100.0 * jax.random.uniform(splits[3], (LAYERS, GRID_ROWS, COLS), jnp.float32) ** levels(splits[3], (LAYERS, GRID_ROWS, COLS), ((0, 4), (1, 32)), -0.2, 0.2), 25.0, 125.0),
        "drop_prior": jnp.clip(1.0 * jax.random.uniform(splits[4], (LAYERS, GRID_ROWS, COLS), jnp.float32) ** levels(splits[4], (LAYERS, GRID_ROWS, COLS), ((0, 4), (1, 32)), -0.2, 0.2), 0.0, 1.0),
        "class_conductance": jnp.clip(jnp.exp(math.log(8.0) - 2.7725887 * jax.random.uniform(splits[5], (LAYERS, CLASSES), jnp.float32) ** levels(splits[5], (LAYERS, CLASSES), ((0, 4),), -0.2, 0.2)), 0.5, 8.0),
    }


centre = 1.0
half_width = 0.9


def harmonic(first, second):
    total = first + second
    safe = jnp.where(total > 0, total, 1.0)
    return jnp.where(total > 0, 2.0 * first * second / safe, 0.0)


def node_conductance(metal_class, table, temp_prior):
    base = jnp.zeros(metal_class.shape, jnp.float32)
    for member in range(table.shape[1]):
        base = base + jnp.where(metal_class == member, table[:, member][:, None, None], 0.0)
    return base / (1.0 + 0.0039 * (temp_prior - 25.0))


def direction_factors(strata):
    along_rows = jnp.where(strata % 2 == 0, 1.0, 0.25).astype(jnp.float32)[:, None, None]
    return along_rows, 1.25 - along_rows


def pad_cols(field):
    return jnp.pad(field, ((0, 0), (0, 0), (1, 1)))


def pad_rows(field):
    return jnp.pad(field, ((0, 0), (1, 1), (0, 0)))


def edge_set(padded_g, along_rows, along_cols, shunt):
    own = padded_g[:, 1:-1]
    north = harmonic(own, padded_g[:, :-2]) * along_rows
    south = harmonic(own, padded_g[:, 2:]) * along_rows
    side = pad_cols(own)
    west = harmonic(own, side[..., :-2]) * along_cols
    east = harmonic(own, side[..., 2:]) * along_cols
    total = north + south + west + east + shunt
    return north, south, west, east, total


def scaled_residual(padded_x, load, edges, safe_total):
    north, south, west, east, total = edges
    own = padded_x[:, 1:-1]
    side = pad_cols(own)
    image = total * own - north * padded_x[:, :-2] - south * padded_x[:, 2:] - west * side[..., :-2] - east * side[..., 2:]
    return (load - image) / safe_total


def joule(padded_x, edges, shunt):
    north, south, west, east, total = edges
    own = padded_x[:, 1:-1]
    side = pad_cols(own)
    heat = north * (own - padded_x[:, :-2]) ** 2 + south * (own - padded_x[:, 2:]) ** 2
    heat = heat + west * (own - side[..., :-2]) ** 2 + east * (own - side[..., 2:]) ** 2
    return 0.1 * (0.5 * heat + shunt * own * own)


def column_solve(heat, vertical_flux):
    node_count = heat.shape[0]
    ratio_values = []
    eliminated_factors = []
    for layer_level in range(node_count):
        pivot_value = 0.2 + vertical_flux[layer_level]
        numerator = heat[layer_level]
        if layer_level > 0:
            pivot_value = pivot_value + vertical_flux[layer_level - 1] - vertical_flux[layer_level - 1] * ratio_values[-1]
            numerator = numerator + vertical_flux[layer_level - 1] * eliminated_factors[-1]
        ratio_values.append(vertical_flux[layer_level] / pivot_value)
        eliminated_factors.append(numerator / pivot_value)
    result_values = [None] * node_count
    result_values[node_count - 1] = eliminated_factors[node_count - 1]
    for layer_level in range(node_count - 2, -1, -1):
        result_values[layer_level] = eliminated_factors[layer_level] + ratio_values[layer_level] * result_values[layer_level + 1]
    return jnp.stack(result_values)


def chebyshev_tail(step_one, drop_one, second):
    rho_one = half_width / centre
    rho_two = 1.0 / (2.0 * centre / half_width - rho_one)
    step_two = rho_two * rho_one * step_one + (2.0 * rho_two / half_width) * second
    return drop_one + step_two


def reference(load_current, metal_class, via_mask, temp_prior, drop_prior, class_conductance):
    strata = jnp.arange(load_current.shape[0], dtype=jnp.int32)
    cond = node_conductance(metal_class, class_conductance, temp_prior)
    along_rows, along_cols = direction_factors(strata)
    vias = via_mask.astype(jnp.float32)
    shunt = cond * (0.05 + 0.5 * vias)
    edges = edge_set(pad_rows(cond), along_rows, along_cols, shunt)
    first = scaled_residual(pad_rows(drop_prior), load_current, edges, edges[4])
    step_one = first / centre
    drop_one = drop_prior + step_one
    second = scaled_residual(pad_rows(drop_one), load_current, edges, edges[4])
    drop_next = chebyshev_tail(step_one, drop_one, second)
    heat = joule(pad_rows(drop_next), edges, shunt)
    vertical_flux = (1.0 + 4.0 * vias) / (1.0 + 0.002 * (temp_prior - 25.0))
    temp_rise = column_solve(heat, vertical_flux)
    return drop_next, temp_rise
```

```python
import functools

import jax
import jax.numpy as jnp
from jax import lax
from jax.experimental import pallas as pl
from jax.experimental.pallas import tpu as pltpu
from jax.sharding import PartitionSpec as P

MESH = pl.DeviceIdType.MESH
F32 = jnp.float32
ROWS = 128
LANES = 128
PAD = 8
HALF_WIDTH = 0.9
RHO_ONE = 0.9
RHO_TWO = 1.0 / (2.0 / HALF_WIDTH - RHO_ONE)
KEEP = RHO_TWO * RHO_ONE
GAIN = 2.0 * RHO_TWO / HALF_WIDTH
ALONG_ROWS = (1.0, 0.25)
ALONG_COLS = (0.25, 1.0)


def rcp(x):
    return pltpu.reciprocal(x, approx=True)


def kernel(
    nt, nl, tiles,
    load_h, cls_h, via_h, temp_h, x0_h, table,
    drop_h, rise_h,
    load, cls, via, temp, x0, x1, x2, res, shunt, inv, east, south, flux, tabs,
    ra, wa, rb, wb, pbuf, nbuf, pin, nin, mid_p, mid_n, t_own, t_far, t_in, t_out,
    h0s, h0r, h1s, h1r, h2s, h2r,
    in_sem, out_sem, hs_sem, hr_sem,
    p_ss, p_rs, n_ss, n_rs, mp_ss, mp_rs, mn_ss, mn_rs, mt_ss, mt_rs, t_ss, t_rs,
):
    d = lax.axis_index("layer")
    tile = lax.axis_index("tile")
    half = tiles // 2
    low = d < nl // 2
    outer = jnp.logical_or(d == 0, d == nl - 1)
    inner = jnp.logical_not(outer)
    lane = lax.broadcasted_iota(jnp.int32, (8, LANES), 1)
    heats = temp

    def order(i):
        j = i + jnp.where(low, half, 0)
        return jnp.where(j >= tiles, j - tiles, j)

    def cols(j):
        return pl.ds(pl.multiple_of(j * LANES, LANES), LANES)

    def fetch(k, j):
        src, dst = (
            (temp_h, temp), (via_h, via), (cls_h, cls), (x0_h, x0), (load_h, load)
        )[k]
        target = dst.at[:, j, pl.ds(PAD, ROWS), :] if k == 3 else dst.at[:, j]
        return pltpu.make_async_copy(src.at[:, :, cols(j)], target, in_sem.at[k, j])

    for ks in ((0, 1), (2,), (3,), (4,)):
        def start_in(i, carry, ks=ks):
            for k in ks:
                fetch(k, order(i)).start()
            return carry
        lax.fori_loop(0, tiles, start_in, 0)

    barrier = pltpu.get_barrier_semaphore()

    def greet(cond, where):
        @pl.when(cond)
        def _():
            pl.semaphore_signal(barrier, inc=1, device_id=where, device_id_type=MESH)

    north_ok = tile > 0
    south_ok = tile < nt - 1
    greet(north_ok, (d, tile - 1))
    greet(south_ok, (d, tile + 1))
    greet(d > 0, (d - 1, tile))
    greet(d < nl - 1, (d + 1, tile))

    tabs[...] = jnp.ones_like(tabs)
    for l in range(2):
        tabs[l, 0:1, 0:16] = 0.5 / table[l : l + 1, :]
        east[l, 0] = jnp.zeros((ROWS, LANES), F32)
        x0[l, tiles] = jnp.zeros((ROWS + 2 * PAD, LANES), F32)
        x1[l, tiles] = jnp.zeros((ROWS + 2 * PAD, LANES), F32)
        x2[l, tiles] = jnp.zeros((ROWS + 2 * PAD, LANES), F32)
        res[l, tiles] = jnp.ones((ROWS + 2 * PAD, LANES), F32)

    @pl.when(tile == 0)
    def _():
        h0r[0, 0:2] = jnp.ones((2, 24, LANES), F32)
        h0r[0, 2:4] = jnp.zeros((2, 24, LANES), F32)
        h1r[0] = jnp.zeros((2, 24, LANES), F32)
        h2r[0] = jnp.zeros((2, 24, LANES), F32)

    @pl.when(tile == nt - 1)
    def _():
        h0r[1, 0:2] = jnp.ones((2, 24, LANES), F32)
        h0r[1, 2:4] = jnp.zeros((2, 24, LANES), F32)
        h1r[1] = jnp.zeros((2, 24, LANES), F32)
        h2r[1] = jnp.zeros((2, 24, LANES), F32)

    pl.semaphore_wait(
        barrier,
        north_ok.astype(jnp.int32) + south_ok.astype(jnp.int32)
        + (d > 0).astype(jnp.int32) + (d < nl - 1).astype(jnp.int32),
    )

    def halo(stage, side, arriving=False):
        up = (side == 0) != arriving
        send, recv = ((h0s, h0r), (h1s, h1r), (h2s, h2r))[stage]
        return pltpu.make_async_remote_copy(
            src_ref=send.at[side], dst_ref=recv.at[1 - side],
            send_sem=hs_sem.at[stage, side], recv_sem=hr_sem.at[stage, 1 - side],
            device_id=(d, tile - 1 if up else tile + 1), device_id_type=MESH,
        )

    def halo_send(stage, fields):
        send = (h0s, h1s, h2s)[stage]

        def pack(j, carry):
            for f, ref in enumerate(fields):
                for l in range(2):
                    send[0, 2 * f + l, pl.ds(j, 1), :] = ref[l, j, PAD : PAD + 1, :]
                    send[1, 2 * f + l, pl.ds(j, 1), :] = ref[l, j, PAD + ROWS - 1 : PAD + ROWS, :]
            return carry

        lax.fori_loop(0, tiles, pack, 0)
        for side, cond in ((0, north_ok), (1, south_ok)):
            @pl.when(cond)
            def _():
                halo(stage, side).start()

    def halo_recv(stage, fields):
        recv = (h0r, h1r, h2r)[stage]
        for side, cond in ((0, north_ok), (1, south_ok)):
            @pl.when(cond)
            def _():
                halo(stage, 1 - side, True).wait_recv()

        def unpack(j, carry):
            for f, ref in enumerate(fields):
                for l in range(2):
                    ref[l, j, PAD - 1 : PAD, :] = recv[0, 2 * f + l, pl.ds(j, 1), :]
                    ref[l, j, PAD + ROWS : PAD + ROWS + 1, :] = recv[1, 2 * f + l, pl.ds(j, 1), :]
            return carry

        lax.fori_loop(0, tiles, unpack, 0)

    def halo_done(stage):
        for side, cond in ((0, north_ok), (1, south_ok)):
            @pl.when(cond)
            def _():
                halo(stage, side).wait_send()

    def toward(i):
        return (jnp.where(low, d + 1, d - 1), tile)

    def away(i):
        return (jnp.where(low, jnp.where(d == 0, d + 1, d - 1), jnp.where(d == nl - 1, d - 1, d + 1)), tile)

    def remote(src, dst, ss, rs, j, where):
        return pltpu.make_async_remote_copy(
            src_ref=src.at[j], dst_ref=dst.at[j], send_sem=ss.at[j], recv_sem=rs.at[j],
            device_id=where, device_id_type=MESH,
        )

    def p_in(i):
        return remote(pbuf, pin, p_ss, p_rs, i, toward(i))

    def n_in(i):
        return remote(nbuf, nin, n_ss, n_rs, i, toward(i))

    def p_mid(i):
        return remote(pbuf, mid_p, mp_ss, mp_rs, i, toward(i))

    def n_mid(i):
        return remote(nbuf, mid_n, mn_ss, mn_rs, i, toward(i))

    def t_mid(i):
        return remote(t_own, t_far, mt_ss, mt_rs, i, toward(i))

    def t_back(i):
        return remote(t_out, t_in, t_ss, t_rs, i, away(i))

    def vertical(l, j, rows):
        up = 1.0 + 4.0 * via[l, j, rows, :].astype(F32)
        return up * rcp(0.95 + 0.002 * temp[l, j, rows, :])

    def matrix(role, i):
        j = order(i)
        for r in range(0, ROWS, 32):
            rows = pl.ds(r, 32)
            v0 = vertical(0, j, rows)
            v1 = vertical(1, j, rows)
            if role == 0:
                da = jnp.full((32, LANES), 0.2, F32)
            elif role == 1:
                da = 0.2 + pin[i, rows, :]
            elif role == 2:
                got = pin[i, rows, :]
                rr = rcp(got + v1)
                wi = v1 * rr
                da = 0.2 + wi * got
                rb[i, rows, :] = rr
                wb[i, rows, :] = wi
            else:
                da = 0.2 + v1
            r_a = rcp(da + v0)
            w_a = v0 * r_a
            ra[i, rows, :] = r_a
            wa[i, rows, :] = w_a
            db = 0.2 + w_a * da
            if role < 2:
                r_b = rcp(db + v1)
                w_b = v1 * r_b
                rb[i, rows, :] = r_b
                wb[i, rows, :] = w_b
                db = w_b * db
            pbuf[i, rows, :] = db

    def outer_matrix(role):
        def body(i, carry):
            fetch(0, order(i)).wait()
            fetch(1, order(i)).wait()
            matrix(role, i)
            p_in(i).start()
            return carry
        lax.fori_loop(0, tiles, body, 0)

    def inner_matrix(role):
        def body(i, carry):
            fetch(1, order(i)).wait()
            p_in(i).wait_recv()
            matrix(role, i)

            @pl.when(i < half)
            def _():
                p_mid(i).start()
            return carry
        lax.fori_loop(0, tiles, body, 0)

    @pl.when(d == 0)
    def _():
        outer_matrix(0)

    @pl.when(d == nl - 1)
    def _():
        outer_matrix(3)

    def resist(i, carry):
        j = order(i)

        @pl.when(inner)
        def _():
            fetch(0, j).wait()
        fetch(2, j).wait()
        for l in range(2):
            look = jnp.broadcast_to(tabs[l, 0:1, :], (8, LANES))
            for r in range(0, ROWS, 8):
                base = jnp.take_along_axis(look, cls[l, j, pl.ds(r, 8), :], axis=1)
                res[l, j, pl.ds(PAD + r, 8), :] = base * (0.9025 + 0.0039 * temp[l, j, pl.ds(r, 8), :])
        fetch(3, j).wait()
        return carry

    lax.fori_loop(0, tiles, resist, 0)
    halo_send(0, (res, x0))

    @pl.when(d == 1)
    def _():
        inner_matrix(1)

    @pl.when(d == 2)
    def _():
        inner_matrix(2)

    def next_col(ref, l, j, rows, own, n):
        mixed = jnp.where(lane_of(n) == 0, ref[l, j + 1, rows, :], own)
        return pltpu.roll(mixed, LANES - 1, 1)

    def lane_of(n):
        return lax.broadcasted_iota(jnp.int32, (n, LANES), 1)

    def prev_col(before, own, n):
        return pltpu.roll(jnp.where(lane_of(n) == LANES - 1, before, own), 1, 1)

    def apply(xref, l, j, r, n, e, s, s_up, g):
        at = pl.ds(PAD + r, n)
        x = xref[l, j, at, :]
        fe = e * (x - next_col(xref, l, j, at, x, n))
        before = flux[l, pl.ds(r, n), :]
        flux[l, pl.ds(r, n), :] = fe
        fs = s * (x - xref[l, j, pl.ds(PAD + r + 1, n), :])
        fn = s_up * (xref[l, j, pl.ds(PAD + r - 1, n), :] - x)
        return x, (fe - prev_col(before, fe, n)) + (fs - fn) + g * x

    def first(j, l, r, n):
        at = pl.ds(PAD + r, n)
        rows = pl.ds(r, n)
        own = res[l, j, at, :]
        e = ALONG_COLS[l] * rcp(own + next_col(res, l, j, at, own, n))
        last = jnp.logical_and(lane_of(n) == LANES - 1, j == tiles - 1)
        e = jnp.where(last, 0.0, e)
        e_before = prev_col(east[l, j, rows, :], e, n)
        east[l, j + 1, rows, :] = e
        s = ALONG_ROWS[l] * rcp(own + res[l, j, pl.ds(PAD + r + 1, n), :])
        s_up = ALONG_ROWS[l] * rcp(own + res[l, j, pl.ds(PAD + r - 1, n), :])
        row = lax.broadcasted_iota(jnp.int32, (n, LANES), 0)
        if r == 0:
            s_up = jnp.where(jnp.logical_and(row == 0, tile == 0), 0.0, s_up)
            south[l, j, PAD - 1 : PAD, :] = s_up[0:1, :]
        if r + n == ROWS:
            s = jnp.where(jnp.logical_and(row == n - 1, tile == nt - 1), 0.0, s)
        south[l, j, at, :] = s
        g = (0.025 + 0.25 * via[l, j, rows, :].astype(F32)) * rcp(own)
        shunt[l, j, rows, :] = g
        iv = rcp(e + e_before + s + s_up + g)
        inv[l, j, rows, :] = iv
        x, ax = apply(x0, l, j, r, n, e, s, s_up, g)
        x1[l, j, at, :] = x + (load[l, j, rows, :] - ax) * iv

    def edges(l, j, r, n):
        return (
            east[l, j + 1, pl.ds(r, n), :],
            south[l, j, pl.ds(PAD + r, n), :],
            south[l, j, pl.ds(PAD + r - 1, n), :],
            shunt[l, j, pl.ds(r, n), :],
        )

    def second(j, l, r, n):
        at = pl.ds(PAD + r, n)
        rows = pl.ds(r, n)
        e, s, s_up, g = edges(l, j, r, n)
        x, ax = apply(x1, l, j, r, n, e, s, s_up, g)
        change = (load[l, j, rows, :] - ax) * inv[l, j, rows, :]
        x2[l, j, at, :] = x + (KEEP * (x - x0[l, j, at, :]) + GAIN * change)

    def heat(j, l, r, n):
        at = pl.ds(PAD + r, n)
        e, s, s_up, g = edges(l, j, r, n)
        x = x2[l, j, at, :]
        de = x - next_col(x2, l, j, at, x, n)
        ds_ = x - x2[l, j, pl.ds(PAD + r + 1, n), :]
        dn = x2[l, j, pl.ds(PAD + r - 1, n), :] - x
        fe = e * de * de
        east_before = east[l, j, pl.ds(r, n), :]
        xb = x2[l, j - 1 + jnp.where(j == 0, 1, 0), at, :]
        dw = x - prev_col(xb, x, n)
        ew = prev_col(east_before, e, n)
        sum_ = (fe + ew * dw * dw) + (s * ds_ * ds_ + s_up * dn * dn)
        heats[l, j, pl.ds(r, n), :] = 0.05 * sum_ + (0.1 * g) * x * x

    def sweep(fn, parts):
        def zero(l):
            flux[l] = jnp.zeros((ROWS, LANES), F32)
        for l in range(2):
            zero(l)

        def body(j, carry):
            for l in range(2):
                for r, n in parts:
                    fn(j, l, r, n)
            return carry
        lax.fori_loop(0, tiles, body, 0)

    rim = ((0, 8), (ROWS - 8, 8))

    def wait_load(j, carry):
        fetch(4, j).wait()
        return carry
    lax.fori_loop(0, tiles, wait_load, 0)
    sweep(first, ((8, 24), (32, 24)))
    halo_recv(0, (res, x0))
    sweep(first, rim)
    halo_send(1, (x1,))
    sweep(first, ((56, 32), (88, 32)))
    halo_recv(1, (x1,))
    sweep(second, rim)
    halo_send(2, (x2,))
    sweep(second, ((8, 32), (40, 32), (72, 24), (96, 24)))
    halo_recv(2, (x2,))

    def drop_out(j):
        return pltpu.make_async_copy(
            x2.at[:, j, pl.ds(PAD, ROWS), :], drop_h.at[:, :, cols(j)], out_sem.at[0, j]
        )

    def rise_out(j):
        return pltpu.make_async_copy(heats.at[:, j], rise_h.at[:, :, cols(j)], out_sem.at[1, j])

    def right_side(role, i):
        j = order(i)
        a, b = (0, 1) if role < 2 else (1, 0)
        for r in range(0, ROWS, 32):
            rows = pl.ds(r, 32)
            na = heats[a, j, rows, :]
            if role == 1:
                na = na + nin[i, rows, :]
                heats[a, j, rows, :] = na
            elif role == 2:
                na = na + wb[i, rows, :] * nin[i, rows, :]
                heats[a, j, rows, :] = na
            nb = heats[b, j, rows, :] + wa[i, rows, :] * na
            heats[b, j, rows, :] = nb
            nbuf[i, rows, :] = wb[i, rows, :] * nb if role < 2 else nb

    def inner_right(i):
        n_in(i).wait_recv()

        @pl.when(d == 1)
        def _():
            right_side(1, i)

        @pl.when(d == 2)
        def _():
            right_side(2, i)

        @pl.when(i < half)
        def _():
            n_mid(i).start()

    def heat_step(i, carry):
        j = order(i)
        drop_out(j).start()
        for l in range(2):
            for r in range(0, ROWS, 32):
                heat(j, l, r, 32)

        @pl.when(d == 0)
        def _():
            right_side(0, i)

        @pl.when(d == nl - 1)
        def _():
            right_side(3, i)

        @pl.when(outer)
        def _():
            n_in(i).start()

        @pl.when(jnp.logical_and(inner, i >= 2))
        def _():
            inner_right(i - 2)
        return carry

    lax.fori_loop(0, tiles, heat_step, 0)

    def back(role, i):
        j = order(i)
        a, b = (0, 1) if role < 2 else (1, 0)
        for r in range(0, ROWS, 32):
            rows = pl.ds(r, 32)
            tin = t_in[i, rows, :]
            tb = heats[b, j, rows, :] * rb[i, rows, :] + wb[i, rows, :] * tin if role < 2 else tin
            ta = heats[a, j, rows, :] * ra[i, rows, :] + wa[i, rows, :] * tb
            heats[b, j, rows, :] = tb
            heats[a, j, rows, :] = ta
            if role == 1:
                t_out[i, rows, :] = ta
            elif role == 2:
                t_out[i, rows, :] = rb[i, rows, :] * nin[i, rows, :] + wb[i, rows, :] * ta
        rise_out(j).start()

    def inner_back(i):
        @pl.when(d == 1)
        def _():
            back(1, i)

        @pl.when(d == 2)
        def _():
            back(2, i)
        t_back(i).start()

    @pl.when(inner)
    def _():
        inner_right(tiles - 2)
        inner_right(tiles - 1)

        def own(k, carry):
            i = half + k
            p_mid(k).wait_recv()
            n_mid(k).wait_recv()
            for r in range(0, ROWS, 32):
                rows = pl.ds(r, 32)
                t4 = (nbuf[i, rows, :] + mid_n[k, rows, :]) * rcp(pbuf[i, rows, :] + mid_p[k, rows, :])
                t_own[k, rows, :] = t4
                t_in[i, rows, :] = t4
            t_mid(k).start()
            inner_back(i)
            return carry
        lax.fori_loop(0, half, own, 0)

        def far(k, carry):
            t_mid(k).wait_recv()
            t_in[k] = t_far[k]
            inner_back(k)
            return carry
        lax.fori_loop(0, half, far, 0)

    @pl.when(outer)
    def _():
        def last(k, carry):
            i = k + half
            i = jnp.where(i >= tiles, i - tiles, i)
            t_back(i).wait_recv()

            @pl.when(d == 0)
            def _():
                back(0, i)

            @pl.when(d == nl - 1)
            def _():
                back(3, i)
            return carry
        lax.fori_loop(0, tiles, last, 0)

    for stage in range(3):
        halo_done(stage)

    def drain(i, carry):
        drop_out(i).wait()
        rise_out(i).wait()

        @pl.when(outer)
        def _():
            p_in(i).wait_send()
            n_in(i).wait_send()

        @pl.when(inner)
        def _():
            t_back(i).wait_send()

        @pl.when(jnp.logical_and(inner, i < half))
        def _():
            p_mid(i).wait_send()
            n_mid(i).wait_send()
            t_mid(i).wait_send()
        return carry
    lax.fori_loop(0, tiles, drain, 0)


def local(nt, nl, load_current, metal_class, via_mask, temp_prior, drop_prior, class_conductance):
    tiles = load_current.shape[2] // LANES
    half = tiles // 2
    wide = ROWS + 2 * PAD
    shape = jax.ShapeDtypeStruct(load_current.shape, F32)
    vm = pltpu.VMEM
    dma = pltpu.SemaphoreType.DMA
    field = vm((2, tiles, ROWS, LANES), F32)
    padded = vm((2, tiles + 1, wide, LANES), F32)
    column = vm((tiles, ROWS, LANES), F32)
    part = vm((half, ROWS, LANES), F32)
    return pl.pallas_call(
        functools.partial(kernel, nt, nl, tiles),
        out_shape=(shape, shape),
        in_specs=[pl.BlockSpec(memory_space=pl.ANY)] * 5 + [pl.BlockSpec(memory_space=pltpu.VMEM)],
        out_specs=[pl.BlockSpec(memory_space=pl.ANY)] * 2,
        scratch_shapes=[
            field,
            vm((2, tiles, ROWS, LANES), jnp.int32),
            vm((2, tiles, ROWS, LANES), jnp.int32),
            field,
            padded, padded, padded, padded,
            field, field,
            vm((2, tiles + 1, ROWS, LANES), F32),
            vm((2, tiles, ROWS + PAD, LANES), F32),
            vm((2, ROWS, LANES), F32),
            vm((2, 8, LANES), F32),
            column, column, column, column,
            column, column, column, column,
            part, part, part, part,
            column, column,
            vm((2, 4, 24, LANES), F32), vm((2, 4, 24, LANES), F32),
            vm((2, 2, 24, LANES), F32), vm((2, 2, 24, LANES), F32),
            vm((2, 2, 24, LANES), F32), vm((2, 2, 24, LANES), F32),
            dma((5, tiles)), dma((2, tiles)), dma((3, 2)), dma((3, 2)),
            dma((tiles,)), dma((tiles,)), dma((tiles,)), dma((tiles,)),
            dma((half,)), dma((half,)), dma((half,)), dma((half,)),
            dma((half,)), dma((half,)), dma((tiles,)), dma((tiles,)),
        ],
        compiler_params=pltpu.CompilerParams(
            collective_id=0, has_side_effects=True, vmem_limit_bytes=63000000
        ),
        cost_estimate=pl.CostEstimate(flops=100000000, bytes_accessed=20200000, transcendentals=5000000),
    )(load_current, metal_class, via_mask, temp_prior, drop_prior, class_conductance)


def solution(mesh):
    in_specs = (
        P("layer", "tile", None),
        P("layer", "tile", None),
        P("layer", "tile", None),
        P("layer", "tile", None),
        P("layer", "tile", None),
        P("layer", None),
    )
    out_specs = (P("layer", "tile", None), P("layer", "tile", None))
    return jax.shard_map(
        functools.partial(local, mesh.shape["tile"], mesh.shape["layer"]),
        mesh=mesh, in_specs=in_specs, out_specs=out_specs, check_vma=False,
    )
```

```python
import functools

import jax
import jax.numpy as jnp
from jax import lax
from jax.experimental import pallas as pl
from jax.experimental.pallas import tpu as pltpu
from jax.sharding import PartitionSpec as P

MESH = pl.DeviceIdType.MESH
F32 = jnp.float32
ROWS = 128
LANES = 128
PAD = 8
HALF_WIDTH = 0.9
RHO_ONE = 0.9
RHO_TWO = 1.0 / (2.0 / HALF_WIDTH - RHO_ONE)
KEEP = RHO_TWO * RHO_ONE
GAIN = 2.0 * RHO_TWO / HALF_WIDTH
ALONG_ROWS = (1.0, 0.25)
ALONG_COLS = (0.25, 1.0)


def rcp(x):
    return pltpu.reciprocal(x, approx=True)


def kernel(
    nt, nl, tiles,
    load_h, cls_h, via_h, temp_h, x0_h, table,
    drop_h, rise_h,
    load, cls, via, temp, x0, x1, x2, res, shunt, inv, east, west, south, tabs,
    ra, wa, rb, wb, pbuf, nbuf, pin, nin, mid_p, mid_n, t_own, t_far, t_in, t_out,
    h0s, h0r, h1s, h1r, h2s, h2r,
    in_sem, out_sem, hs_sem, hr_sem,
    p_ss, p_rs, n_ss, n_rs, mp_ss, mp_rs, mn_ss, mn_rs, mt_ss, mt_rs, t_ss, t_rs,
):
    d = lax.axis_index("layer")
    tile = lax.axis_index("tile")
    half = tiles // 2
    low = d < nl // 2
    outer = jnp.logical_or(d == 0, d == nl - 1)
    inner = jnp.logical_not(outer)
    heats = temp

    def order(i):
        j = i + jnp.where(low, half, 0)
        return jnp.where(j >= tiles, j - tiles, j)

    def cols(j):
        return pl.ds(pl.multiple_of(j * LANES, LANES), LANES)

    def fetch(k, j):
        src, dst = (
            (temp_h, temp), (via_h, via), (cls_h, cls), (x0_h, x0), (load_h, load)
        )[k]
        target = dst.at[:, j, pl.ds(PAD, ROWS), :] if k == 3 else dst.at[:, j]
        return pltpu.make_async_copy(src.at[:, :, cols(j)], target, in_sem.at[k, j])

    for ks in ((0, 1), (2,), (3,), (4,)):
        def start_in(i, carry, ks=ks):
            for k in ks:
                fetch(k, order(i)).start()
            return carry
        lax.fori_loop(0, tiles, start_in, 0)

    barrier = pltpu.get_barrier_semaphore()

    def greet(cond, where):
        @pl.when(cond)
        def _():
            pl.semaphore_signal(barrier, inc=1, device_id=where, device_id_type=MESH)

    north_ok = tile > 0
    south_ok = tile < nt - 1
    greet(north_ok, (d, tile - 1))
    greet(south_ok, (d, tile + 1))
    greet(d > 0, (d - 1, tile))
    greet(d < nl - 1, (d + 1, tile))

    tabs[...] = jnp.ones_like(tabs)
    for l in range(2):
        tabs[l, 0:1, 0:16] = 0.5 / table[l : l + 1, :]

    @pl.when(tile == 0)
    def _():
        h0r[0, 0:2] = jnp.ones((2, 24, LANES), F32)
        h0r[0, 2:4] = jnp.zeros((2, 24, LANES), F32)
        h1r[0] = jnp.zeros((2, 24, LANES), F32)
        h2r[0] = jnp.zeros((2, 24, LANES), F32)

    @pl.when(tile == nt - 1)
    def _():
        h0r[1, 0:2] = jnp.ones((2, 24, LANES), F32)
        h0r[1, 2:4] = jnp.zeros((2, 24, LANES), F32)
        h1r[1] = jnp.zeros((2, 24, LANES), F32)
        h2r[1] = jnp.zeros((2, 24, LANES), F32)

    pl.semaphore_wait(
        barrier,
        north_ok.astype(jnp.int32) + south_ok.astype(jnp.int32)
        + (d > 0).astype(jnp.int32) + (d < nl - 1).astype(jnp.int32),
    )

    def halo(stage, side, arriving=False):
        up = (side == 0) != arriving
        send, recv = ((h0s, h0r), (h1s, h1r), (h2s, h2r))[stage]
        return pltpu.make_async_remote_copy(
            src_ref=send.at[side], dst_ref=recv.at[1 - side],
            send_sem=hs_sem.at[stage, side], recv_sem=hr_sem.at[stage, 1 - side],
            device_id=(d, tile - 1 if up else tile + 1), device_id_type=MESH,
        )

    def halo_send(stage, fields):
        send = (h0s, h1s, h2s)[stage]

        def pack(j, carry):
            for f, ref in enumerate(fields):
                for l in range(2):
                    send[0, 2 * f + l, pl.ds(j, 1), :] = ref[l, j, PAD : PAD + 1, :]
                    send[1, 2 * f + l, pl.ds(j, 1), :] = ref[l, j, PAD + ROWS - 1 : PAD + ROWS, :]
            return carry

        lax.fori_loop(0, tiles, pack, 0)
        for side, cond in ((0, north_ok), (1, south_ok)):
            @pl.when(cond)
            def _():
                halo(stage, side).start()

    def halo_recv(stage, fields):
        recv = (h0r, h1r, h2r)[stage]
        for side, cond in ((0, north_ok), (1, south_ok)):
            @pl.when(cond)
            def _():
                halo(stage, 1 - side, True).wait_recv()

        def unpack(j, carry):
            for f, ref in enumerate(fields):
                for l in range(2):
                    ref[l, j, PAD - 1 : PAD, :] = recv[0, 2 * f + l, pl.ds(j, 1), :]
                    ref[l, j, PAD + ROWS : PAD + ROWS + 1, :] = recv[1, 2 * f + l, pl.ds(j, 1), :]
            return carry

        lax.fori_loop(0, tiles, unpack, 0)

    def halo_done(stage):
        for side, cond in ((0, north_ok), (1, south_ok)):
            @pl.when(cond)
            def _():
                halo(stage, side).wait_send()

    def toward(i):
        return (jnp.where(low, d + 1, d - 1), tile)

    def away(i):
        return (jnp.where(low, jnp.where(d == 0, d + 1, d - 1), jnp.where(d == nl - 1, d - 1, d + 1)), tile)

    def remote(src, dst, ss, rs, j, where):
        return pltpu.make_async_remote_copy(
            src_ref=src.at[j], dst_ref=dst.at[j], send_sem=ss.at[j], recv_sem=rs.at[j],
            device_id=where, device_id_type=MESH,
        )

    def p_in(i):
        return remote(pbuf, pin, p_ss, p_rs, i, toward(i))

    def n_in(i):
        return remote(nbuf, nin, n_ss, n_rs, i, toward(i))

    def p_mid(i):
        return remote(pbuf, mid_p, mp_ss, mp_rs, i, toward(i))

    def n_mid(i):
        return remote(nbuf, mid_n, mn_ss, mn_rs, i, toward(i))

    def t_mid(i):
        return remote(t_own, t_far, mt_ss, mt_rs, i, toward(i))

    def t_back(i):
        return remote(t_out, t_in, t_ss, t_rs, i, away(i))

    def vertical(l, j, rows):
        up = 1.0 + 4.0 * via[l, j, rows, :].astype(F32)
        return up * rcp(0.95 + 0.002 * temp[l, j, rows, :])

    def matrix(role, i):
        j = order(i)
        for r in range(0, ROWS, 32):
            rows = pl.ds(r, 32)
            v0 = vertical(0, j, rows)
            v1 = vertical(1, j, rows)
            if role == 0:
                da = jnp.full((32, LANES), 0.2, F32)
            elif role == 1:
                da = 0.2 + pin[i, rows, :]
            elif role == 2:
                got = pin[i, rows, :]
                rr = rcp(got + v1)
                wi = v1 * rr
                da = 0.2 + wi * got
                rb[i, rows, :] = rr
                wb[i, rows, :] = wi
            else:
                da = 0.2 + v1
            r_a = rcp(da + v0)
            w_a = v0 * r_a
            ra[i, rows, :] = r_a
            wa[i, rows, :] = w_a
            db = 0.2 + w_a * da
            if role < 2:
                r_b = rcp(db + v1)
                w_b = v1 * r_b
                rb[i, rows, :] = r_b
                wb[i, rows, :] = w_b
                db = w_b * db
            pbuf[i, rows, :] = db

    def outer_matrix(role):
        def body(i, carry):
            fetch(0, order(i)).wait()
            fetch(1, order(i)).wait()
            matrix(role, i)
            p_in(i).start()
            return carry
        lax.fori_loop(0, tiles, body, 0)

    def inner_matrix(role):
        def body(i, carry):
            fetch(0, order(i)).wait()
            fetch(1, order(i)).wait()
            p_in(i).wait_recv()
            matrix(role, i)

            @pl.when(i < half)
            def _():
                p_mid(i).start()
            return carry
        lax.fori_loop(0, tiles, body, 0)

    @pl.when(d == 0)
    def _():
        outer_matrix(0)

    @pl.when(d == nl - 1)
    def _():
        outer_matrix(3)

    @pl.when(d == 1)
    def _():
        inner_matrix(1)

    @pl.when(d == 2)
    def _():
        inner_matrix(2)

    def resist(i, carry):
        j = order(i)
        fetch(2, j).wait()
        for l in range(2):
            look = jnp.broadcast_to(tabs[l, 0:1, :], (8, LANES))
            for r in range(0, ROWS, 8):
                base = jnp.take_along_axis(look, cls[l, j, pl.ds(r, 8), :], axis=1)
                res[l, j, pl.ds(PAD + r, 8), :] = base * (0.9025 + 0.0039 * temp[l, j, pl.ds(r, 8), :])
        fetch(3, j).wait()
        return carry

    lax.fori_loop(0, tiles, resist, 0)
    halo_send(0, (res, x0))

    def lane_of(n):
        return lax.broadcasted_iota(jnp.int32, (n, LANES), 1)

    def next_col(ref, l, j, rows, own, n):
        side = ref[l, jnp.where(j == tiles - 1, j, j + 1), rows, :]
        return pltpu.roll(jnp.where(lane_of(n) == 0, side, own), LANES - 1, 1)

    def prev_col(ref, l, j, rows, own, n):
        side = ref[l, jnp.where(j == 0, j, j - 1), rows, :]
        return pltpu.roll(jnp.where(lane_of(n) == LANES - 1, side, own), 1, 1)

    def differences(xref, l, j, r, n):
        at = pl.ds(PAD + r, n)
        x = xref[l, j, at, :]
        return (
            x,
            x - next_col(xref, l, j, at, x, n),
            x - prev_col(xref, l, j, at, x, n),
            x - xref[l, j, pl.ds(PAD + r + 1, n), :],
            x - xref[l, j, pl.ds(PAD + r - 1, n), :],
        )

    def apply(xref, l, j, r, n, e, w, s, s_up, g):
        x, de, dw, ds_, dn = differences(xref, l, j, r, n)
        return x, (e * de + w * dw) + (s * ds_ + s_up * dn) + g * x

    def first(j, l, r, n):
        at = pl.ds(PAD + r, n)
        rows = pl.ds(r, n)
        own = res[l, j, at, :]
        lanes = lane_of(n)
        e = ALONG_COLS[l] * rcp(own + next_col(res, l, j, at, own, n))
        e = jnp.where(jnp.logical_and(lanes == LANES - 1, j == tiles - 1), 0.0, e)
        w = ALONG_COLS[l] * rcp(own + prev_col(res, l, j, at, own, n))
        w = jnp.where(jnp.logical_and(lanes == 0, j == 0), 0.0, w)
        s = ALONG_ROWS[l] * rcp(own + res[l, j, pl.ds(PAD + r + 1, n), :])
        s_up = ALONG_ROWS[l] * rcp(own + res[l, j, pl.ds(PAD + r - 1, n), :])
        row = lax.broadcasted_iota(jnp.int32, (n, LANES), 0)
        if r == 0:
            s_up = jnp.where(jnp.logical_and(row == 0, tile == 0), 0.0, s_up)
            south[l, j, PAD - 1 : PAD, :] = s_up[0:1, :]
        if r + n == ROWS:
            s = jnp.where(jnp.logical_and(row == n - 1, tile == nt - 1), 0.0, s)
        g = (0.025 + 0.25 * via[l, j, rows, :].astype(F32)) * rcp(own)
        iv = rcp((e + w) + (s + s_up) + g)
        x, ax = apply(x0, l, j, r, n, e, w, s, s_up, g)
        x1[l, j, at, :] = x + (load[l, j, rows, :] - ax) * iv
        east[l, j, rows, :] = e
        west[l, j, rows, :] = w
        south[l, j, at, :] = s
        shunt[l, j, rows, :] = g
        inv[l, j, rows, :] = iv

    def edges(l, j, r, n):
        return (
            east[l, j, pl.ds(r, n), :],
            west[l, j, pl.ds(r, n), :],
            south[l, j, pl.ds(PAD + r, n), :],
            south[l, j, pl.ds(PAD + r - 1, n), :],
            shunt[l, j, pl.ds(r, n), :],
        )

    def second(j, l, r, n):
        at = pl.ds(PAD + r, n)
        rows = pl.ds(r, n)
        x, ax = apply(x1, l, j, r, n, *edges(l, j, r, n))
        change = (load[l, j, rows, :] - ax) * inv[l, j, rows, :]
        x2[l, j, at, :] = x + (KEEP * (x - x0[l, j, at, :]) + GAIN * change)

    def heat(j, l, r, n):
        e, w, s, s_up, g = edges(l, j, r, n)
        x, de, dw, ds_, dn = differences(x2, l, j, r, n)
        total = (e * de * de + w * dw * dw) + (s * ds_ * ds_ + s_up * dn * dn)
        heats[l, j, pl.ds(r, n), :] = 0.05 * total + (0.1 * g) * x * x

    def sweep(fn, parts, unroll):
        unroll = max(k for k in range(1, unroll + 1) if tiles % k == 0)

        def body(k, carry):
            for u in range(unroll):
                for l in range(2):
                    for r, n in parts:
                        fn(k * unroll + u, l, r, n)
            return carry
        lax.fori_loop(0, tiles // unroll, body, 0)

    rim = ((0, 8), (ROWS - 8, 8))

    def wait_load(j, carry):
        fetch(4, j).wait()
        return carry
    lax.fori_loop(0, tiles, wait_load, 0)
    sweep(first, ((8, 24), (32, 24)), 11)
    halo_recv(0, (res, x0))
    sweep(first, rim, 11)
    halo_send(1, (x1,))
    sweep(first, ((56, 32), (88, 32)), 11)
    halo_recv(1, (x1,))
    sweep(second, rim, 11)
    halo_send(2, (x2,))
    sweep(second, ((8, 32), (40, 32), (72, 24), (96, 24)), 11)
    halo_recv(2, (x2,))

    def drop_out(j):
        return pltpu.make_async_copy(
            x2.at[:, j, pl.ds(PAD, ROWS), :], drop_h.at[:, :, cols(j)], out_sem.at[0, j]
        )

    def rise_out(j):
        return pltpu.make_async_copy(heats.at[:, j], rise_h.at[:, :, cols(j)], out_sem.at[1, j])

    def right_side(role, i):
        j = order(i)
        a, b = (0, 1) if role < 2 else (1, 0)
        for r in range(0, ROWS, 32):
            rows = pl.ds(r, 32)
            na = heats[a, j, rows, :]
            if role == 1:
                na = na + nin[i, rows, :]
                heats[a, j, rows, :] = na
            elif role == 2:
                na = na + wb[i, rows, :] * nin[i, rows, :]
                heats[a, j, rows, :] = na
            nb = heats[b, j, rows, :] + wa[i, rows, :] * na
            heats[b, j, rows, :] = nb
            nbuf[i, rows, :] = wb[i, rows, :] * nb if role < 2 else nb

    def inner_right(i):
        n_in(i).wait_recv()

        @pl.when(d == 1)
        def _():
            right_side(1, i)

        @pl.when(d == 2)
        def _():
            right_side(2, i)

        @pl.when(i < half)
        def _():
            n_mid(i).start()

    def heat_step(i, carry):
        j = order(i)
        drop_out(j).start()
        for l in range(2):
            for r in range(0, ROWS, 32):
                heat(j, l, r, 32)

        @pl.when(d == 0)
        def _():
            right_side(0, i)

        @pl.when(d == nl - 1)
        def _():
            right_side(3, i)

        @pl.when(outer)
        def _():
            n_in(i).start()

        @pl.when(jnp.logical_and(inner, i >= 2))
        def _():
            inner_right(i - 2)
        return carry

    lax.fori_loop(0, tiles, heat_step, 0)

    def back(role, i):
        j = order(i)
        a, b = (0, 1) if role < 2 else (1, 0)
        for r in range(0, ROWS, 32):
            rows = pl.ds(r, 32)
            tin = t_in[i, rows, :]
            tb = heats[b, j, rows, :] * rb[i, rows, :] + wb[i, rows, :] * tin if role < 2 else tin
            ta = heats[a, j, rows, :] * ra[i, rows, :] + wa[i, rows, :] * tb
            heats[b, j, rows, :] = tb
            heats[a, j, rows, :] = ta
            if role == 1:
                t_out[i, rows, :] = ta
            elif role == 2:
                t_out[i, rows, :] = rb[i, rows, :] * nin[i, rows, :] + wb[i, rows, :] * ta
        rise_out(j).start()

    def inner_back(i):
        @pl.when(d == 1)
        def _():
            back(1, i)

        @pl.when(d == 2)
        def _():
            back(2, i)
        t_back(i).start()

    @pl.when(inner)
    def _():
        inner_right(tiles - 2)
        inner_right(tiles - 1)

        def own(k, carry):
            i = half + k
            p_mid(k).wait_recv()
            n_mid(k).wait_recv()
            for r in range(0, ROWS, 32):
                rows = pl.ds(r, 32)
                t4 = (nbuf[i, rows, :] + mid_n[k, rows, :]) * rcp(pbuf[i, rows, :] + mid_p[k, rows, :])
                t_own[k, rows, :] = t4
                t_in[i, rows, :] = t4
            t_mid(k).start()
            inner_back(i)
            return carry
        lax.fori_loop(0, half, own, 0)

        def far(k, carry):
            t_mid(k).wait_recv()
            t_in[k] = t_far[k]
            inner_back(k)
            return carry
        lax.fori_loop(0, half, far, 0)

    @pl.when(outer)
    def _():
        def last(k, carry):
            i = k + half
            i = jnp.where(i >= tiles, i - tiles, i)
            t_back(i).wait_recv()

            @pl.when(d == 0)
            def _():
                back(0, i)

            @pl.when(d == nl - 1)
            def _():
                back(3, i)
            return carry
        lax.fori_loop(0, tiles, last, 0)

    for stage in range(3):
        halo_done(stage)

    def drain(i, carry):
        drop_out(i).wait()
        rise_out(i).wait()

        @pl.when(outer)
        def _():
            p_in(i).wait_send()
            n_in(i).wait_send()

        @pl.when(inner)
        def _():
            t_back(i).wait_send()

        @pl.when(jnp.logical_and(inner, i < half))
        def _():
            p_mid(i).wait_send()
            n_mid(i).wait_send()
            t_mid(i).wait_send()
        return carry
    lax.fori_loop(0, tiles, drain, 0)


def local(nt, nl, load_current, metal_class, via_mask, temp_prior, drop_prior, class_conductance):
    tiles = load_current.shape[2] // LANES
    half = tiles // 2
    wide = ROWS + 2 * PAD
    shape = jax.ShapeDtypeStruct(load_current.shape, F32)
    vm = pltpu.VMEM
    dma = pltpu.SemaphoreType.DMA
    field = vm((2, tiles, ROWS, LANES), F32)
    padded = vm((2, tiles, wide, LANES), F32)
    column = vm((tiles, ROWS, LANES), F32)
    part = vm((half, ROWS, LANES), F32)
    return pl.pallas_call(
        functools.partial(kernel, nt, nl, tiles),
        out_shape=(shape, shape),
        in_specs=[pl.BlockSpec(memory_space=pl.ANY)] * 5 + [pl.BlockSpec(memory_space=pltpu.VMEM)],
        out_specs=[pl.BlockSpec(memory_space=pl.ANY)] * 2,
        scratch_shapes=[
            field,
            vm((2, tiles, ROWS, LANES), jnp.int32),
            vm((2, tiles, ROWS, LANES), jnp.int32),
            field,
            padded, padded, padded, padded,
            field, field,
            field, field,
            vm((2, tiles, ROWS + PAD, LANES), F32),
                vm((2, 8, LANES), F32),
            column, column, column, column,
            column, column, column, column,
            part, part, part, part,
            column, column,
            vm((2, 4, 24, LANES), F32), vm((2, 4, 24, LANES), F32),
            vm((2, 2, 24, LANES), F32), vm((2, 2, 24, LANES), F32),
            vm((2, 2, 24, LANES), F32), vm((2, 2, 24, LANES), F32),
            dma((5, tiles)), dma((2, tiles)), dma((3, 2)), dma((3, 2)),
            dma((tiles,)), dma((tiles,)), dma((tiles,)), dma((tiles,)),
            dma((half,)), dma((half,)), dma((half,)), dma((half,)),
            dma((half,)), dma((half,)), dma((tiles,)), dma((tiles,)),
        ],
        compiler_params=pltpu.CompilerParams(
            collective_id=0, has_side_effects=True, vmem_limit_bytes=63000000
        ),
        cost_estimate=pl.CostEstimate(flops=100000000, bytes_accessed=20200000, transcendentals=5000000),
    )(load_current, metal_class, via_mask, temp_prior, drop_prior, class_conductance)


def solution(mesh):
    in_specs = (
        P("layer", "tile", None),
        P("layer", "tile", None),
        P("layer", "tile", None),
        P("layer", "tile", None),
        P("layer", "tile", None),
        P("layer", None),
    )
    out_specs = (P("layer", "tile", None), P("layer", "tile", None))
    return jax.shard_map(
        functools.partial(local, mesh.shape["tile"], mesh.shape["layer"]),
        mesh=mesh, in_specs=in_specs, out_specs=out_specs, check_vma=False,
    )
```

```python
import functools

import jax
import jax.numpy as jnp
from jax import lax
from jax.experimental import pallas as pl
from jax.experimental.pallas import tpu as pltpu
from jax.sharding import PartitionSpec as P

MESH = pl.DeviceIdType.MESH
F32 = jnp.float32
ROWS = 128
LANES = 128
PAD = 8
HALF_WIDTH = 0.9
RHO_ONE = 0.9
RHO_TWO = 1.0 / (2.0 / HALF_WIDTH - RHO_ONE)
KEEP = RHO_TWO * RHO_ONE
GAIN = 2.0 * RHO_TWO / HALF_WIDTH
ALONG_ROWS = (1.0, 0.25)
ALONG_COLS = (0.25, 1.0)


def rcp(x):
    return pltpu.reciprocal(x, approx=True)


def kernel(
    nt, nl, tiles,
    load_h, cls_h, via_h, temp_h, x0_h, table,
    drop_h, rise_h,
    load, cls, via, temp, x0, x1, x2, res, shunt, inv, east, west, south, tabs,
    ra, wa, rb, wb, pbuf, nbuf, pin, nin, mid_p, mid_n, t_own, t_far, t_in, t_out,
    h0s, h0r, h1s, h1r, h2s, h2r,
    temp_rim, cls_rim, x0_rim, rim_sem, in_sem, out_sem, hs_sem, hr_sem,
    p_ss, p_rs, n_ss, n_rs, mp_ss, mp_rs, mn_ss, mn_rs, mt_ss, mt_rs, t_ss, t_rs,
):
    d = lax.axis_index("layer")
    tile = lax.axis_index("tile")
    half = tiles // 2
    low = d < nl // 2
    outer = jnp.logical_or(d == 0, d == nl - 1)
    inner = jnp.logical_not(outer)
    heats = temp

    def order(i):
        j = i + jnp.where(low, half, 0)
        return jnp.where(j >= tiles, j - tiles, j)

    def cols(j):
        return pl.ds(pl.multiple_of(j * LANES, LANES), LANES)

    def fetch(k, j):
        src, dst = (
            (temp_h, temp), (via_h, via), (cls_h, cls), (x0_h, x0), (load_h, load)
        )[k]
        target = dst.at[:, j, pl.ds(PAD, ROWS), :] if k == 3 else dst.at[:, j]
        return pltpu.make_async_copy(src.at[:, :, cols(j)], target, in_sem.at[k, j])

    def fetch_rim(k, side):
        src, dst = ((temp_h, temp_rim), (cls_h, cls_rim), (x0_h, x0_rim))[k]
        return pltpu.make_async_copy(
            src.at[:, pl.ds(side * (ROWS - 8), 8), :], dst.at[side], rim_sem.at[k, side]
        )

    for k in range(3):
        for side in range(2):
            fetch_rim(k, side).start()

    def start_in(i, carry):
        fetch(0, order(i)).start()
        fetch(1, order(i)).start()
        return carry
    lax.fori_loop(0, tiles, start_in, 0)

    barrier = pltpu.get_barrier_semaphore()

    def greet(cond, where):
        @pl.when(cond)
        def _():
            pl.semaphore_signal(barrier, inc=1, device_id=where, device_id_type=MESH)

    north_ok = tile > 0
    south_ok = tile < nt - 1
    greet(north_ok, (d, tile - 1))
    greet(south_ok, (d, tile + 1))
    greet(d > 0, (d - 1, tile))
    greet(d < nl - 1, (d + 1, tile))

    tabs[...] = jnp.ones_like(tabs)
    for l in range(2):
        tabs[l, 0:1, 0:16] = 0.5 / table[l : l + 1, :]

    @pl.when(tile == 0)
    def _():
        h0r[0, 0:2] = jnp.ones((2, 24, LANES), F32)
        h0r[0, 2:4] = jnp.zeros((2, 24, LANES), F32)
        h1r[0] = jnp.zeros((2, 24, LANES), F32)
        h2r[0] = jnp.zeros((2, 24, LANES), F32)

    @pl.when(tile == nt - 1)
    def _():
        h0r[1, 0:2] = jnp.ones((2, 24, LANES), F32)
        h0r[1, 2:4] = jnp.zeros((2, 24, LANES), F32)
        h1r[1] = jnp.zeros((2, 24, LANES), F32)
        h2r[1] = jnp.zeros((2, 24, LANES), F32)

    for k in range(3):
        for side in range(2):
            fetch_rim(k, side).wait()

    def rim_pack(j, carry):
        for side in range(2):
            row = 7 * side
            for l in range(2):
                look = jnp.broadcast_to(tabs[l, 0:1, :], (8, LANES))
                base = jnp.take_along_axis(look, cls_rim[side, l, :, cols(j)], axis=1)
                own = base * (0.9025 + 0.0039 * temp_rim[side, l, :, cols(j)])
                h0s[side, l, pl.ds(j, 1), :] = own[row : row + 1, :]
                h0s[side, 2 + l, pl.ds(j, 1), :] = x0_rim[side, l, row : row + 1, cols(j)]
        return carry
    lax.fori_loop(0, tiles, rim_pack, 0)

    pl.semaphore_wait(
        barrier,
        north_ok.astype(jnp.int32) + south_ok.astype(jnp.int32)
        + (d > 0).astype(jnp.int32) + (d < nl - 1).astype(jnp.int32),
    )

    def halo(stage, side, arriving=False):
        up = (side == 0) != arriving
        send, recv = ((h0s, h0r), (h1s, h1r), (h2s, h2r))[stage]
        return pltpu.make_async_remote_copy(
            src_ref=send.at[side], dst_ref=recv.at[1 - side],
            send_sem=hs_sem.at[stage, side], recv_sem=hr_sem.at[stage, 1 - side],
            device_id=(d, tile - 1 if up else tile + 1), device_id_type=MESH,
        )

    def halo_start(stage):
        for side, cond in ((0, north_ok), (1, south_ok)):
            @pl.when(cond)
            def _():
                halo(stage, side).start()

    def halo_send(stage, fields):
        send = (h0s, h1s, h2s)[stage]

        def pack(j, carry):
            for f, ref in enumerate(fields):
                for l in range(2):
                    send[0, 2 * f + l, pl.ds(j, 1), :] = ref[l, j, PAD : PAD + 1, :]
                    send[1, 2 * f + l, pl.ds(j, 1), :] = ref[l, j, PAD + ROWS - 1 : PAD + ROWS, :]
            return carry

        lax.fori_loop(0, tiles, pack, 0)
        halo_start(stage)

    def halo_recv(stage, fields):
        recv = (h0r, h1r, h2r)[stage]
        for side, cond in ((0, north_ok), (1, south_ok)):
            @pl.when(cond)
            def _():
                halo(stage, 1 - side, True).wait_recv()

        def unpack(j, carry):
            for f, ref in enumerate(fields):
                for l in range(2):
                    ref[l, j, PAD - 1 : PAD, :] = recv[0, 2 * f + l, pl.ds(j, 1), :]
                    ref[l, j, PAD + ROWS : PAD + ROWS + 1, :] = recv[1, 2 * f + l, pl.ds(j, 1), :]
            return carry

        lax.fori_loop(0, tiles, unpack, 0)

    def halo_done(stage):
        for side, cond in ((0, north_ok), (1, south_ok)):
            @pl.when(cond)
            def _():
                halo(stage, side).wait_send()

    halo_start(0)

    def toward(i):
        return (jnp.where(low, d + 1, d - 1), tile)

    def away(i):
        return (jnp.where(low, jnp.where(d == 0, d + 1, d - 1), jnp.where(d == nl - 1, d - 1, d + 1)), tile)

    def remote(src, dst, ss, rs, j, where):
        return pltpu.make_async_remote_copy(
            src_ref=src.at[j], dst_ref=dst.at[j], send_sem=ss.at[j], recv_sem=rs.at[j],
            device_id=where, device_id_type=MESH,
        )

    def p_in(i):
        return remote(pbuf, pin, p_ss, p_rs, i, toward(i))

    def n_in(i):
        return remote(nbuf, nin, n_ss, n_rs, i, toward(i))

    def p_mid(i):
        return remote(pbuf, mid_p, mp_ss, mp_rs, i, toward(i))

    def n_mid(i):
        return remote(nbuf, mid_n, mn_ss, mn_rs, i, toward(i))

    def t_mid(i):
        return remote(t_own, t_far, mt_ss, mt_rs, i, toward(i))

    def t_back(i):
        return remote(t_out, t_in, t_ss, t_rs, i, away(i))

    def vertical(l, j, rows):
        up = 1.0 + 4.0 * via[l, j, rows, :].astype(F32)
        return up * rcp(0.95 + 0.002 * temp[l, j, rows, :])

    def matrix(role, i):
        j = order(i)
        for r in range(0, ROWS, 32):
            rows = pl.ds(r, 32)
            v0 = vertical(0, j, rows)
            v1 = vertical(1, j, rows)
            if role == 0:
                da = jnp.full((32, LANES), 0.2, F32)
            elif role == 1:
                da = 0.2 + pin[i, rows, :]
            elif role == 2:
                got = pin[i, rows, :]
                rr = rcp(got + v1)
                wi = v1 * rr
                da = 0.2 + wi * got
                rb[i, rows, :] = rr
                wb[i, rows, :] = wi
            else:
                da = 0.2 + v1
            r_a = rcp(da + v0)
            w_a = v0 * r_a
            ra[i, rows, :] = r_a
            wa[i, rows, :] = w_a
            db = 0.2 + w_a * da
            if role < 2:
                r_b = rcp(db + v1)
                w_b = v1 * r_b
                rb[i, rows, :] = r_b
                wb[i, rows, :] = w_b
                db = w_b * db
            pbuf[i, rows, :] = db

    def start_rest(i):
        for k in (2, 3, 4):
            fetch(k, order(i)).start()

    def outer_matrix(role):
        def body(i, carry):
            fetch(0, order(i)).wait()
            fetch(1, order(i)).wait()
            matrix(role, i)
            p_in(i).start()
            start_rest(i)
            return carry
        lax.fori_loop(0, tiles, body, 0)

    def inner_matrix(role):
        def body(i, carry):
            start_rest(i)
            fetch(0, order(i)).wait()
            fetch(1, order(i)).wait()
            p_in(i).wait_recv()
            matrix(role, i)

            @pl.when(i < half)
            def _():
                p_mid(i).start()
            return carry
        lax.fori_loop(0, tiles, body, 0)

    @pl.when(d == 0)
    def _():
        outer_matrix(0)

    @pl.when(d == nl - 1)
    def _():
        outer_matrix(3)

    @pl.when(d == 1)
    def _():
        inner_matrix(1)

    @pl.when(d == 2)
    def _():
        inner_matrix(2)

    def resist(i, carry):
        j = order(i)
        fetch(2, j).wait()
        for l in range(2):
            look = jnp.broadcast_to(tabs[l, 0:1, :], (8, LANES))
            for r in range(0, ROWS, 8):
                base = jnp.take_along_axis(look, cls[l, j, pl.ds(r, 8), :], axis=1)
                res[l, j, pl.ds(PAD + r, 8), :] = base * (0.9025 + 0.0039 * temp[l, j, pl.ds(r, 8), :])
        fetch(3, j).wait()
        return carry

    lax.fori_loop(0, tiles, resist, 0)

    def lane_of(n):
        return lax.broadcasted_iota(jnp.int32, (n, LANES), 1)

    def next_col(ref, l, j, rows, own, n):
        side = ref[l, jnp.where(j == tiles - 1, j, j + 1), rows, :]
        return pltpu.roll(jnp.where(lane_of(n) == 0, side, own), LANES - 1, 1)

    def prev_col(ref, l, j, rows, own, n):
        side = ref[l, jnp.where(j == 0, j, j - 1), rows, :]
        return pltpu.roll(jnp.where(lane_of(n) == LANES - 1, side, own), 1, 1)

    def differences(xref, l, j, r, n):
        at = pl.ds(PAD + r, n)
        x = xref[l, j, at, :]
        return (
            x,
            x - next_col(xref, l, j, at, x, n),
            x - prev_col(xref, l, j, at, x, n),
            x - xref[l, j, pl.ds(PAD + r + 1, n), :],
            x - xref[l, j, pl.ds(PAD + r - 1, n), :],
        )

    def apply(xref, l, j, r, n, e, w, s, s_up, g):
        x, de, dw, ds_, dn = differences(xref, l, j, r, n)
        return x, (e * de + w * dw) + (s * ds_ + s_up * dn) + g * x

    def first(j, l, r, n):
        at = pl.ds(PAD + r, n)
        rows = pl.ds(r, n)
        own = res[l, j, at, :]
        lanes = lane_of(n)
        e = ALONG_COLS[l] * rcp(own + next_col(res, l, j, at, own, n))
        e = jnp.where(jnp.logical_and(lanes == LANES - 1, j == tiles - 1), 0.0, e)
        w = ALONG_COLS[l] * rcp(own + prev_col(res, l, j, at, own, n))
        w = jnp.where(jnp.logical_and(lanes == 0, j == 0), 0.0, w)
        s = ALONG_ROWS[l] * rcp(own + res[l, j, pl.ds(PAD + r + 1, n), :])
        s_up = ALONG_ROWS[l] * rcp(own + res[l, j, pl.ds(PAD + r - 1, n), :])
        row = lax.broadcasted_iota(jnp.int32, (n, LANES), 0)
        if r == 0:
            s_up = jnp.where(jnp.logical_and(row == 0, tile == 0), 0.0, s_up)
            south[l, j, PAD - 1 : PAD, :] = s_up[0:1, :]
        if r + n == ROWS:
            s = jnp.where(jnp.logical_and(row == n - 1, tile == nt - 1), 0.0, s)
        g = (0.025 + 0.25 * via[l, j, rows, :].astype(F32)) * rcp(own)
        iv = rcp((e + w) + (s + s_up) + g)
        x, ax = apply(x0, l, j, r, n, e, w, s, s_up, g)
        x1[l, j, at, :] = x + (load[l, j, rows, :] - ax) * iv
        east[l, j, rows, :] = e
        west[l, j, rows, :] = w
        south[l, j, at, :] = s
        shunt[l, j, rows, :] = g
        inv[l, j, rows, :] = iv

    def edges(l, j, r, n):
        return (
            east[l, j, pl.ds(r, n), :],
            west[l, j, pl.ds(r, n), :],
            south[l, j, pl.ds(PAD + r, n), :],
            south[l, j, pl.ds(PAD + r - 1, n), :],
            shunt[l, j, pl.ds(r, n), :],
        )

    def second(j, l, r, n):
        at = pl.ds(PAD + r, n)
        rows = pl.ds(r, n)
        x, ax = apply(x1, l, j, r, n, *edges(l, j, r, n))
        change = (load[l, j, rows, :] - ax) * inv[l, j, rows, :]
        x2[l, j, at, :] = x + (KEEP * (x - x0[l, j, at, :]) + GAIN * change)

    def heat(j, l, r, n):
        e, w, s, s_up, g = edges(l, j, r, n)
        x, de, dw, ds_, dn = differences(x2, l, j, r, n)
        total = (e * de * de + w * dw * dw) + (s * ds_ * ds_ + s_up * dn * dn)
        heats[l, j, pl.ds(r, n), :] = 0.05 * total + (0.1 * g) * x * x

    def sweep(fn, parts, unroll):
        unroll = max(k for k in range(1, unroll + 1) if tiles % k == 0)

        def body(k, carry):
            for u in range(unroll):
                for l in range(2):
                    for r, n in parts:
                        fn(k * unroll + u, l, r, n)
            return carry
        lax.fori_loop(0, tiles // unroll, body, 0)

    rim = ((0, 8), (ROWS - 8, 8))
    middle = ((8, 32), (40, 32), (72, 24), (96, 24))

    def wait_load(j, carry):
        fetch(4, j).wait()
        return carry
    lax.fori_loop(0, tiles, wait_load, 0)
    halo_recv(0, (res, x0))
    sweep(first, rim, 11)
    halo_send(1, (x1,))
    sweep(first, middle, 11)
    halo_recv(1, (x1,))
    sweep(second, rim, 11)
    halo_send(2, (x2,))
    sweep(second, middle, 11)
    sweep(heat, middle, 11)
    halo_recv(2, (x2,))
    sweep(heat, rim, 11)

    def drop_out(j):
        return pltpu.make_async_copy(
            x2.at[:, j, pl.ds(PAD, ROWS), :], drop_h.at[:, :, cols(j)], out_sem.at[0, j]
        )

    def rise_out(j):
        return pltpu.make_async_copy(heats.at[:, j], rise_h.at[:, :, cols(j)], out_sem.at[1, j])

    def right_side(role, i):
        j = order(i)
        a, b = (0, 1) if role < 2 else (1, 0)
        for r in range(0, ROWS, 32):
            rows = pl.ds(r, 32)
            na = heats[a, j, rows, :]
            if role == 1:
                na = na + nin[i, rows, :]
                heats[a, j, rows, :] = na
            elif role == 2:
                na = na + wb[i, rows, :] * nin[i, rows, :]
                heats[a, j, rows, :] = na
            nb = heats[b, j, rows, :] + wa[i, rows, :] * na
            heats[b, j, rows, :] = nb
            nbuf[i, rows, :] = wb[i, rows, :] * nb if role < 2 else nb

    def inner_right(i):
        n_in(i).wait_recv()

        @pl.when(d == 1)
        def _():
            right_side(1, i)

        @pl.when(d == 2)
        def _():
            right_side(2, i)

        @pl.when(i < half)
        def _():
            n_mid(i).start()

    def heat_step(i, carry):
        j = order(i)
        drop_out(j).start()

        @pl.when(d == 0)
        def _():
            right_side(0, i)

        @pl.when(d == nl - 1)
        def _():
            right_side(3, i)

        @pl.when(outer)
        def _():
            n_in(i).start()

        @pl.when(jnp.logical_and(inner, i >= 2))
        def _():
            inner_right(i - 2)
        return carry

    lax.fori_loop(0, tiles, heat_step, 0)

    def back(role, i):
        j = order(i)
        a, b = (0, 1) if role < 2 else (1, 0)
        for r in range(0, ROWS, 32):
            rows = pl.ds(r, 32)
            tin = t_in[i, rows, :]
            tb = heats[b, j, rows, :] * rb[i, rows, :] + wb[i, rows, :] * tin if role < 2 else tin
            ta = heats[a, j, rows, :] * ra[i, rows, :] + wa[i, rows, :] * tb
            heats[b, j, rows, :] = tb
            heats[a, j, rows, :] = ta
            if role == 1:
                t_out[i, rows, :] = ta
            elif role == 2:
                t_out[i, rows, :] = rb[i, rows, :] * nin[i, rows, :] + wb[i, rows, :] * ta
        rise_out(j).start()

    def inner_back(i):
        @pl.when(d == 1)
        def _():
            back(1, i)

        @pl.when(d == 2)
        def _():
            back(2, i)
        t_back(i).start()

    @pl.when(inner)
    def _():
        inner_right(tiles - 2)
        inner_right(tiles - 1)

        def own(k, carry):
            i = half + k
            p_mid(k).wait_recv()
            n_mid(k).wait_recv()
            for r in range(0, ROWS, 32):
                rows = pl.ds(r, 32)
                t4 = (nbuf[i, rows, :] + mid_n[k, rows, :]) * rcp(pbuf[i, rows, :] + mid_p[k, rows, :])
                t_own[k, rows, :] = t4
                t_in[i, rows, :] = t4
            t_mid(k).start()
            inner_back(i)
            return carry
        lax.fori_loop(0, half, own, 0)

        def far(k, carry):
            t_mid(k).wait_recv()
            t_in[k] = t_far[k]
            inner_back(k)
            return carry
        lax.fori_loop(0, half, far, 0)

    @pl.when(outer)
    def _():
        def last(k, carry):
            i = k + half
            i = jnp.where(i >= tiles, i - tiles, i)
            t_back(i).wait_recv()

            @pl.when(d == 0)
            def _():
                back(0, i)

            @pl.when(d == nl - 1)
            def _():
                back(3, i)
            return carry
        lax.fori_loop(0, tiles, last, 0)

    for stage in range(3):
        halo_done(stage)

    def drain(i, carry):
        drop_out(i).wait()
        rise_out(i).wait()

        @pl.when(outer)
        def _():
            p_in(i).wait_send()
            n_in(i).wait_send()

        @pl.when(inner)
        def _():
            t_back(i).wait_send()

        @pl.when(jnp.logical_and(inner, i < half))
        def _():
            p_mid(i).wait_send()
            n_mid(i).wait_send()
            t_mid(i).wait_send()
        return carry
    lax.fori_loop(0, tiles, drain, 0)


def local(nt, nl, load_current, metal_class, via_mask, temp_prior, drop_prior, class_conductance):
    tiles = load_current.shape[2] // LANES
    half = tiles // 2
    wide = ROWS + 2 * PAD
    shape = jax.ShapeDtypeStruct(load_current.shape, F32)
    vm = pltpu.VMEM
    dma = pltpu.SemaphoreType.DMA
    field = vm((2, tiles, ROWS, LANES), F32)
    padded = vm((2, tiles, wide, LANES), F32)
    column = vm((tiles, ROWS, LANES), F32)
    part = vm((half, ROWS, LANES), F32)
    return pl.pallas_call(
        functools.partial(kernel, nt, nl, tiles),
        out_shape=(pltpu.VMEM(load_current.shape, F32), pltpu.VMEM(load_current.shape, F32)),
        in_specs=[pl.BlockSpec(memory_space=pl.ANY)] * 5 + [pl.BlockSpec(memory_space=pltpu.VMEM)],
        out_specs=[pl.BlockSpec(memory_space=pltpu.VMEM)] * 2,
        scratch_shapes=[
            field,
            vm((2, tiles, ROWS, LANES), jnp.int32),
            vm((2, tiles, ROWS, LANES), jnp.int32),
            field,
            padded, padded, padded, padded,
            field, field,
            field, field,
            vm((2, tiles, ROWS + PAD, LANES), F32),
                vm((2, 8, LANES), F32),
            column, column, column, column,
            column, column, column, column,
            part, part, part, part,
            column, column,
            vm((2, 4, 24, LANES), F32), vm((2, 4, 24, LANES), F32),
            vm((2, 2, 24, LANES), F32), vm((2, 2, 24, LANES), F32),
            vm((2, 2, 24, LANES), F32), vm((2, 2, 24, LANES), F32),
            vm((2, 2, 8, tiles * LANES), F32), vm((2, 2, 8, tiles * LANES), jnp.int32),
            vm((2, 2, 8, tiles * LANES), F32), dma((3, 2)), dma((5, tiles)), dma((2, tiles)), dma((3, 2)), dma((3, 2)),
            dma((tiles,)), dma((tiles,)), dma((tiles,)), dma((tiles,)),
            dma((half,)), dma((half,)), dma((half,)), dma((half,)),
            dma((half,)), dma((half,)), dma((tiles,)), dma((tiles,)),
        ],
        compiler_params=pltpu.CompilerParams(
            collective_id=0, has_side_effects=True, vmem_limit_bytes=59000000
        ),
        cost_estimate=pl.CostEstimate(flops=100000000, bytes_accessed=20200000, transcendentals=5000000),
    )(load_current, metal_class, via_mask, temp_prior, drop_prior, class_conductance)


def solution(mesh):
    in_specs = (
        P("layer", "tile", None),
        P("layer", "tile", None),
        P("layer", "tile", None),
        P("layer", "tile", None),
        P("layer", "tile", None),
        P("layer", None),
    )
    out_specs = (P("layer", "tile", None), P("layer", "tile", None))
    return jax.shard_map(
        functools.partial(local, mesh.shape["tile"], mesh.shape["layer"]),
        mesh=mesh, in_specs=in_specs, out_specs=out_specs, check_vma=False,
    )
```

```python
import functools

import jax
import jax.numpy as jnp
from jax import lax
from jax.experimental import pallas as pl
from jax.experimental.pallas import tpu as pltpu
from jax.sharding import PartitionSpec as P

MESH = pl.DeviceIdType.MESH
F32 = jnp.float32
ROWS = 128
LANES = 128
CHAINS = 64
PAD = 8
HALF_WIDTH = 0.9
RHO_ONE = 0.9
RHO_TWO = 1.0 / (2.0 / HALF_WIDTH - RHO_ONE)
KEEP = RHO_TWO * RHO_ONE
GAIN = 2.0 * RHO_TWO / HALF_WIDTH
ALONG_ROWS = (1.0, 0.25)
ALONG_COLS = (0.25, 1.0)


def rcp(x):
    return pltpu.reciprocal(x, approx=True)


def kernel(
    nt, nl, tiles,
    load_h, cls_h, via_h, temp_h, x0_h, table,
    drop_h, rise_h,
    load, cls, via, temp, x0, x1, x2, res, shunt, inv, east, west, south, tabs,
    ra, wa, rb, wb, pbuf, nbuf, pin, nin, mid_p, mid_n, t_own, t_far, t_in, t_out,
    h0s, h0r, h1s, h1r, h2s, h2r,
    temp_rim, cls_rim, x0_rim, rim_sem, in_sem, out_sem, hs_sem, hr_sem,
    p_ss, p_rs, n_ss, n_rs, mp_ss, mp_rs, mn_ss, mn_rs, mt_ss, mt_rs, t_ss, t_rs,
):
    d = lax.axis_index("layer")
    tile = lax.axis_index("tile")
    half = tiles // 2
    early = half // 3 + 1
    low = d < nl // 2
    outer = jnp.logical_or(d == 0, d == nl - 1)
    inner = jnp.logical_not(outer)
    heats = temp

    def order(i):
        return jnp.where(low, tiles - 1 - i, i)

    def cols(j):
        return pl.ds(pl.multiple_of(j * LANES, LANES), LANES)

    def fetch(k, j):
        src, dst = (
            (temp_h, temp), (via_h, via), (cls_h, cls), (x0_h, x0), (load_h, load)
        )[k]
        target = dst.at[:, j, pl.ds(PAD, ROWS), :] if k == 3 else dst.at[:, j]
        return pltpu.make_async_copy(src.at[:, :, cols(j)], target, in_sem.at[k, j])

    def fetch_rim(k, side):
        src, dst = ((temp_h, temp_rim), (cls_h, cls_rim), (x0_h, x0_rim))[k]
        return pltpu.make_async_copy(
            src.at[:, pl.ds(side * (ROWS - 8), 8), :], dst.at[side], rim_sem.at[k, side]
        )

    for k in range(3):
        for side in range(2):
            fetch_rim(k, side).start()

    def start_in(i, carry):
        fetch(0, order(i)).start()
        fetch(1, order(i)).start()
        return carry
    lax.fori_loop(0, tiles, start_in, 0)

    barrier = pltpu.get_barrier_semaphore()

    def greet(cond, where):
        @pl.when(cond)
        def _():
            pl.semaphore_signal(barrier, inc=1, device_id=where, device_id_type=MESH)

    north_ok = tile > 0
    south_ok = tile < nt - 1
    greet(north_ok, (d, tile - 1))
    greet(south_ok, (d, tile + 1))
    greet(d > 0, (d - 1, tile))
    greet(d < nl - 1, (d + 1, tile))

    tabs[...] = jnp.ones_like(tabs)
    for l in range(2):
        tabs[l, 0:1, 0:16] = 0.5 / table[l : l + 1, :]

    @pl.when(tile == 0)
    def _():
        h0r[0, 0:2] = jnp.ones((2, 24, LANES), F32)
        h0r[0, 2:4] = jnp.zeros((2, 24, LANES), F32)
        h1r[0] = jnp.zeros((2, 24, LANES), F32)
        h2r[0] = jnp.zeros((2, 24, LANES), F32)

    @pl.when(tile == nt - 1)
    def _():
        h0r[1, 0:2] = jnp.ones((2, 24, LANES), F32)
        h0r[1, 2:4] = jnp.zeros((2, 24, LANES), F32)
        h1r[1] = jnp.zeros((2, 24, LANES), F32)
        h2r[1] = jnp.zeros((2, 24, LANES), F32)

    for k in range(3):
        for side in range(2):
            fetch_rim(k, side).wait()

    def rim_pack(i, carry):
        j = order(i)
        for side in range(2):
            row = 7 * side
            for l in range(2):
                look = jnp.broadcast_to(tabs[l, 0:1, :], (8, LANES))
                base = jnp.take_along_axis(look, cls_rim[side, l, :, cols(j)], axis=1)
                own = base * (0.9025 + 0.0039 * temp_rim[side, l, :, cols(j)])
                h0s[side, l, pl.ds(i, 1), :] = own[row : row + 1, :]
                h0s[side, 2 + l, pl.ds(i, 1), :] = x0_rim[side, l, row : row + 1, cols(j)]
        return carry
    lax.fori_loop(0, tiles, rim_pack, 0)

    pl.semaphore_wait(
        barrier,
        north_ok.astype(jnp.int32) + south_ok.astype(jnp.int32)
        + (d > 0).astype(jnp.int32) + (d < nl - 1).astype(jnp.int32),
    )

    def halo(stage, side, arriving=False):
        up = (side == 0) != arriving
        send, recv = ((h0s, h0r), (h1s, h1r), (h2s, h2r))[stage]
        return pltpu.make_async_remote_copy(
            src_ref=send.at[side], dst_ref=recv.at[1 - side],
            send_sem=hs_sem.at[stage, side], recv_sem=hr_sem.at[stage, 1 - side],
            device_id=(d, tile - 1 if up else tile + 1), device_id_type=MESH,
        )

    def halo_start(stage):
        for side, cond in ((0, north_ok), (1, south_ok)):
            @pl.when(cond)
            def _():
                halo(stage, side).start()

    def halo_send(stage, fields, lo, hi):
        send = (h0s, h1s, h2s)[stage]

        def pack(i, carry):
            j = order(i)
            for f, ref in enumerate(fields):
                for l in range(2):
                    send[0, 2 * f + l, pl.ds(i - lo, 1), :] = ref[l, j, PAD : PAD + 1, :]
                    send[1, 2 * f + l, pl.ds(i - lo, 1), :] = ref[l, j, PAD + ROWS - 1 : PAD + ROWS, :]
            return carry

        lax.fori_loop(lo, hi, pack, 0)
        halo_start(stage)

    def halo_recv(stage, fields, lo, hi):
        recv = (h0r, h1r, h2r)[stage]
        for side, cond in ((0, north_ok), (1, south_ok)):
            @pl.when(cond)
            def _():
                halo(stage, 1 - side, True).wait_recv()

        def unpack(i, carry):
            j = order(i)
            for f, ref in enumerate(fields):
                for l in range(2):
                    ref[l, j, PAD - 1 : PAD, :] = recv[0, 2 * f + l, pl.ds(i - lo, 1), :]
                    ref[l, j, PAD + ROWS : PAD + ROWS + 1, :] = recv[1, 2 * f + l, pl.ds(i - lo, 1), :]
            return carry

        lax.fori_loop(lo, hi, unpack, 0)

    def halo_done(stage):
        for side, cond in ((0, north_ok), (1, south_ok)):
            @pl.when(cond)
            def _():
                halo(stage, side).wait_send()

    halo_start(0)

    def toward(i):
        return (jnp.where(low, d + 1, d - 1), tile)

    def away(i):
        return (jnp.where(low, jnp.where(d == 0, d + 1, d - 1), jnp.where(d == nl - 1, d - 1, d + 1)), tile)

    def remote(src, dst, ss, rs, j, where, to=None):
        k = j if to is None else to
        return pltpu.make_async_remote_copy(
            src_ref=src.at[j], dst_ref=dst.at[k], send_sem=ss.at[j], recv_sem=rs.at[k],
            device_id=where, device_id_type=MESH,
        )

    def p_in(i):
        return remote(pbuf, pin, p_ss, p_rs, i, toward(i))

    def n_in(i):
        return remote(nbuf, nin, n_ss, n_rs, i, toward(i))

    def p_mid(i):
        return remote(pbuf, mid_p, mp_ss, mp_rs, i, toward(i), half - 1 - i)

    def n_mid(i):
        return remote(nbuf, mid_n, mn_ss, mn_rs, i, toward(i), half - 1 - i)

    def t_mid(i):
        return remote(t_own, t_far, mt_ss, mt_rs, i, toward(i), half - 1 - i)

    def t_back(i):
        return remote(t_out, t_in, t_ss, t_rs, i, away(i))

    def vertical(l, j, rows):
        up = 1.0 + 4.0 * via[l, j, rows, :].astype(F32)
        return up * rcp(0.95 + 0.002 * temp[l, j, rows, :])

    def matrix(role, i):
        j = order(i)
        for r in range(0, ROWS, 32):
            rows = pl.ds(r, 32)
            v0 = vertical(0, j, rows)
            v1 = vertical(1, j, rows)
            if role == 0:
                da = jnp.full((32, LANES), 0.2, F32)
            elif role == 1:
                da = 0.2 + pin[i, rows, :]
            elif role == 2:
                got = pin[i, rows, :]
                rr = rcp(got + v1)
                wi = v1 * rr
                da = 0.2 + wi * got
                rb[i, rows, :] = rr
                wb[i, rows, :] = wi
            else:
                da = 0.2 + v1
            r_a = rcp(da + v0)
            w_a = v0 * r_a
            ra[i, rows, :] = r_a
            wa[i, rows, :] = w_a
            db = 0.2 + w_a * da
            if role < 2:
                r_b = rcp(db + v1)
                w_b = v1 * r_b
                rb[i, rows, :] = r_b
                wb[i, rows, :] = w_b
                db = w_b * db
            pbuf[i, rows, :] = db

    def start_rest(i):
        for k in (2, 3, 4):
            fetch(k, order(i)).start()

    def outer_matrix(role):
        def body(i, carry):
            fetch(0, order(i)).wait()
            fetch(1, order(i)).wait()
            matrix(role, i)
            p_in(i).start()
            start_rest(i)
            return carry
        lax.fori_loop(0, tiles, body, 0)

    def inner_matrix(role):
        def body(i, carry):
            start_rest(i)
            fetch(0, order(i)).wait()
            fetch(1, order(i)).wait()
            p_in(i).wait_recv()
            matrix(role, i)

            @pl.when(i < early)
            def _():
                p_mid(i).start()
            return carry
        lax.fori_loop(0, tiles, body, 0)

    @pl.when(d == 0)
    def _():
        outer_matrix(0)

    @pl.when(d == nl - 1)
    def _():
        outer_matrix(3)

    @pl.when(d == 1)
    def _():
        inner_matrix(1)

    @pl.when(d == 2)
    def _():
        inner_matrix(2)

    def resist(i, carry):
        j = order(i)
        fetch(2, j).wait()
        for l in range(2):
            look = jnp.broadcast_to(tabs[l, 0:1, :], (8, LANES))
            for r in range(0, ROWS, 8):
                base = jnp.take_along_axis(look, cls[l, j, pl.ds(r, 8), :], axis=1)
                res[l, j, pl.ds(PAD + r, 8), :] = base * (0.9025 + 0.0039 * temp[l, j, pl.ds(r, 8), :])
        fetch(3, j).wait()
        return carry

    lax.fori_loop(0, tiles, resist, 0)

    def lane_of(n):
        return lax.broadcasted_iota(jnp.int32, (n, LANES), 1)

    def next_col(ref, l, j, rows, own, n):
        side = ref[l, jnp.where(j == tiles - 1, j, j + 1), rows, :]
        return pltpu.roll(jnp.where(lane_of(n) == 0, side, own), LANES - 1, 1)

    def prev_col(ref, l, j, rows, own, n):
        side = ref[l, jnp.where(j == 0, j, j - 1), rows, :]
        return pltpu.roll(jnp.where(lane_of(n) == LANES - 1, side, own), 1, 1)

    def differences(xref, l, j, r, n):
        at = pl.ds(PAD + r, n)
        x = xref[l, j, at, :]
        return (
            x,
            x - next_col(xref, l, j, at, x, n),
            x - prev_col(xref, l, j, at, x, n),
            x - xref[l, j, pl.ds(PAD + r + 1, n), :],
            x - xref[l, j, pl.ds(PAD + r - 1, n), :],
        )

    def apply(xref, l, j, r, n, e, w, s, s_up, g):
        x, de, dw, ds_, dn = differences(xref, l, j, r, n)
        return x, (e * de + w * dw) + (s * ds_ + s_up * dn) + g * x

    def first(j, l, r, n):
        at = pl.ds(PAD + r, n)
        rows = pl.ds(r, n)
        own = res[l, j, at, :]
        lanes = lane_of(n)
        e = ALONG_COLS[l] * rcp(own + next_col(res, l, j, at, own, n))
        e = jnp.where(jnp.logical_and(lanes == LANES - 1, j == tiles - 1), 0.0, e)
        w = ALONG_COLS[l] * rcp(own + prev_col(res, l, j, at, own, n))
        w = jnp.where(jnp.logical_and(lanes == 0, j == 0), 0.0, w)
        s = ALONG_ROWS[l] * rcp(own + res[l, j, pl.ds(PAD + r + 1, n), :])
        s_up = ALONG_ROWS[l] * rcp(own + res[l, j, pl.ds(PAD + r - 1, n), :])
        row = lax.broadcasted_iota(jnp.int32, (n, LANES), 0)
        if r == 0:
            s_up = jnp.where(jnp.logical_and(row == 0, tile == 0), 0.0, s_up)
            south[l, j, PAD - 1 : PAD, :] = s_up[0:1, :]
        if r + n == ROWS:
            s = jnp.where(jnp.logical_and(row == n - 1, tile == nt - 1), 0.0, s)
        g = (0.025 + 0.25 * via[l, j, rows, :].astype(F32)) * rcp(own)
        iv = rcp((e + w) + (s + s_up) + g)
        x, ax = apply(x0, l, j, r, n, e, w, s, s_up, g)
        x1[l, j, at, :] = x + (load[l, j, rows, :] - ax) * iv
        east[l, j, rows, :] = e
        west[l, j, rows, :] = w
        south[l, j, at, :] = s
        shunt[l, j, rows, :] = g
        inv[l, j, rows, :] = iv

    def edges(l, j, r, n):
        return (
            east[l, j, pl.ds(r, n), :],
            west[l, j, pl.ds(r, n), :],
            south[l, j, pl.ds(PAD + r, n), :],
            south[l, j, pl.ds(PAD + r - 1, n), :],
            shunt[l, j, pl.ds(r, n), :],
        )

    def second(j, l, r, n):
        at = pl.ds(PAD + r, n)
        rows = pl.ds(r, n)
        x, ax = apply(x1, l, j, r, n, *edges(l, j, r, n))
        change = (load[l, j, rows, :] - ax) * inv[l, j, rows, :]
        x2[l, j, at, :] = x + (KEEP * (x - x0[l, j, at, :]) + GAIN * change)

    def heat(j, l, r, n):
        e, w, s, s_up, g = edges(l, j, r, n)
        x, de, dw, ds_, dn = differences(x2, l, j, r, n)
        total = (e * de * de + w * dw * dw) + (s * ds_ * ds_ + s_up * dn * dn)
        heats[l, j, pl.ds(r, n), :] = 0.05 * total + (0.1 * g) * x * x

    def sweep(fn, parts, lo, hi):
        unroll = max(1, min(hi - lo, CHAINS // (2 * sum(n for _, n in parts) // 8)))
        full = (hi - lo) // unroll

        def step(start, count):
            for u in range(count):
                j = order(start + u)
                for l in range(2):
                    for r, n in parts:
                        fn(j, l, r, n)

        def body(k, carry):
            step(lo + k * unroll, unroll)
            return carry
        lax.fori_loop(0, full, body, 0)
        if lo + full * unroll < hi:
            step(lo + full * unroll, hi - lo - full * unroll)

    rim = ((0, 8), (ROWS - 8, 8))
    core = ((16, 32), (48, 32), (80, 32))
    middle = ((8, 32), (40, 32), (72, 24), (96, 24))

    def drop_out(j):
        return pltpu.make_async_copy(
            x2.at[:, j, pl.ds(PAD, ROWS), :], drop_h.at[:, :, cols(j)], out_sem.at[0, j]
        )

    def rise_out(j):
        return pltpu.make_async_copy(heats.at[:, j], rise_h.at[:, :, cols(j)], out_sem.at[1, j])

    def right_side(role, i):
        j = order(i)
        a, b = (0, 1) if role < 2 else (1, 0)
        for r in range(0, ROWS, 32):
            rows = pl.ds(r, 32)
            na = heats[a, j, rows, :]
            if role == 1:
                na = na + nin[i, rows, :]
                heats[a, j, rows, :] = na
            elif role == 2:
                na = na + wb[i, rows, :] * nin[i, rows, :]
                heats[a, j, rows, :] = na
            nb = heats[b, j, rows, :] + wa[i, rows, :] * na
            heats[b, j, rows, :] = nb
            nbuf[i, rows, :] = wb[i, rows, :] * nb if role < 2 else nb

    def right_outer(lo, hi):
        for role, where in ((0, 0), (3, nl - 1)):
            @pl.when(d == where)
            def _(role=role):
                def body(i, carry):
                    right_side(role, i)
                    n_in(i).start()
                    return carry
                lax.fori_loop(lo, hi, body, 0)

    def right_inner(lo, hi):
        for role in (1, 2):
            @pl.when(d == role)
            def _(role=role):
                def body(i, carry):
                    n_in(i).wait_recv()
                    right_side(role, i)
                    if hi <= half:
                        n_mid(i).start()
                    return carry
                lax.fori_loop(lo, hi, body, 0)

    def wait_load(j, carry):
        fetch(4, j).wait()
        return carry

    def start_drop(j, carry):
        drop_out(j).start()
        return carry

    two = min(half + 3, tiles)
    one = min(half + 1, tiles)
    lax.fori_loop(0, tiles, wait_load, 0)
    halo_recv(0, (res, x0), 0, tiles)
    sweep(first, ((0, 16), (ROWS - 16, 16)), 0, tiles)
    halo_send(1, (x1,), 0, tiles)

    @pl.when(inner)
    def _():
        def send_rest(i, carry):
            p_mid(i).start()
            return carry
        lax.fori_loop(early, half, send_rest, 0)

    sweep(first, core, 0, two)
    halo_recv(1, (x1,), 0, tiles)
    sweep(second, rim, 0, tiles)
    halo_send(2, (x2,), 0, tiles)
    sweep(second, middle, 0, one)
    sweep(heat, middle, 0, half)
    halo_recv(2, (x2,), 0, tiles)
    sweep(heat, rim, 0, half)
    right_outer(0, half)
    sweep(first, core, two, (two + tiles) // 2)
    right_inner(0, half)
    sweep(first, core, (two + tiles) // 2, tiles)
    sweep(second, middle, one, tiles)
    sweep(heat, rim + middle, half, tiles)
    lax.fori_loop(0, tiles, start_drop, 0)
    right_outer(half, tiles)
    right_inner(half, tiles)

    def back(role, i):
        j = order(i)
        a, b = (0, 1) if role < 2 else (1, 0)
        for r in range(0, ROWS, 32):
            rows = pl.ds(r, 32)
            tin = t_in[i, rows, :]
            tb = heats[b, j, rows, :] * rb[i, rows, :] + wb[i, rows, :] * tin if role < 2 else tin
            ta = heats[a, j, rows, :] * ra[i, rows, :] + wa[i, rows, :] * tb
            heats[b, j, rows, :] = tb
            heats[a, j, rows, :] = ta
            if role == 1:
                t_out[i, rows, :] = ta
            elif role == 2:
                t_out[i, rows, :] = rb[i, rows, :] * nin[i, rows, :] + wb[i, rows, :] * ta
        rise_out(j).start()

    def inner_back(i):
        @pl.when(d == 1)
        def _():
            back(1, i)

        @pl.when(d == 2)
        def _():
            back(2, i)
        t_back(i).start()

    @pl.when(inner)
    def _():
        def own(kk, carry):
            k = half - 1 - kk
            i = half + k
            p_mid(kk).wait_recv()
            n_mid(kk).wait_recv()
            for r in range(0, ROWS, 32):
                rows = pl.ds(r, 32)
                t4 = (nbuf[i, rows, :] + mid_n[k, rows, :]) * rcp(pbuf[i, rows, :] + mid_p[k, rows, :])
                t_own[k, rows, :] = t4
                t_in[i, rows, :] = t4
            t_mid(k).start()
            inner_back(i)
            return carry
        lax.fori_loop(0, half, own, 0)

        def far(k, carry):
            t_mid(half - 1 - k).wait_recv()
            t_in[k] = t_far[k]
            inner_back(k)
            return carry
        lax.fori_loop(0, half, far, 0)

    @pl.when(outer)
    def _():
        def last(k, carry):
            i = jnp.where(k < half, tiles - 1 - k, k - half)
            t_back(i).wait_recv()

            @pl.when(d == 0)
            def _():
                back(0, i)

            @pl.when(d == nl - 1)
            def _():
                back(3, i)
            return carry
        lax.fori_loop(0, tiles, last, 0)

    for stage in range(3):
        halo_done(stage)

    def drain(i, carry):
        drop_out(i).wait()
        rise_out(i).wait()

        @pl.when(outer)
        def _():
            p_in(i).wait_send()
            n_in(i).wait_send()

        @pl.when(inner)
        def _():
            t_back(i).wait_send()

        @pl.when(jnp.logical_and(inner, i < half))
        def _():
            p_mid(i).wait_send()
            n_mid(i).wait_send()
            t_mid(i).wait_send()
        return carry
    lax.fori_loop(0, tiles, drain, 0)


def local(nt, nl, load_current, metal_class, via_mask, temp_prior, drop_prior, class_conductance):
    tiles = load_current.shape[2] // LANES
    half = tiles // 2
    wide = ROWS + 2 * PAD
    shape = jax.ShapeDtypeStruct(load_current.shape, F32)
    vm = pltpu.VMEM
    dma = pltpu.SemaphoreType.DMA
    field = vm((2, tiles, ROWS, LANES), F32)
    padded = vm((2, tiles, wide, LANES), F32)
    column = vm((tiles, ROWS, LANES), F32)
    part = vm((half, ROWS, LANES), F32)
    return pl.pallas_call(
        functools.partial(kernel, nt, nl, tiles),
        out_shape=(pltpu.VMEM(load_current.shape, F32), pltpu.VMEM(load_current.shape, F32)),
        in_specs=[pl.BlockSpec(memory_space=pl.ANY)] * 5 + [pl.BlockSpec(memory_space=pltpu.VMEM)],
        out_specs=[pl.BlockSpec(memory_space=pltpu.VMEM)] * 2,
        scratch_shapes=[
            field,
            vm((2, tiles, ROWS, LANES), jnp.int32),
            vm((2, tiles, ROWS, LANES), jnp.int32),
            field,
            padded, padded, padded, padded,
            field, field,
            field, field,
            vm((2, tiles, ROWS + PAD, LANES), F32),
                vm((2, 8, LANES), F32),
            column, column, column, column,
            column, column, column, column,
            part, part, part, part,
            column, column,
            vm((2, 4, 24, LANES), F32), vm((2, 4, 24, LANES), F32),
            vm((2, 2, 24, LANES), F32), vm((2, 2, 24, LANES), F32),
            vm((2, 2, 24, LANES), F32), vm((2, 2, 24, LANES), F32),
            vm((2, 2, 8, tiles * LANES), F32), vm((2, 2, 8, tiles * LANES), jnp.int32),
            vm((2, 2, 8, tiles * LANES), F32), dma((3, 2)), dma((5, tiles)), dma((2, tiles)), dma((3, 2)), dma((3, 2)),
            dma((tiles,)), dma((tiles,)), dma((tiles,)), dma((tiles,)),
            dma((half,)), dma((half,)), dma((half,)), dma((half,)),
            dma((half,)), dma((half,)), dma((tiles,)), dma((tiles,)),
        ],
        compiler_params=pltpu.CompilerParams(
            collective_id=0, has_side_effects=True, vmem_limit_bytes=59000000
        ),
        cost_estimate=pl.CostEstimate(flops=100000000, bytes_accessed=20200000, transcendentals=5000000),
    )(load_current, metal_class, via_mask, temp_prior, drop_prior, class_conductance)


def solution(mesh):
    in_specs = (
        P("layer", "tile", None),
        P("layer", "tile", None),
        P("layer", "tile", None),
        P("layer", "tile", None),
        P("layer", "tile", None),
        P("layer", None),
    )
    out_specs = (P("layer", "tile", None), P("layer", "tile", None))
    return jax.shard_map(
        functools.partial(local, mesh.shape["tile"], mesh.shape["layer"]),
        mesh=mesh, in_specs=in_specs, out_specs=out_specs, check_vma=False,
    )
```
